32 devices in a mesh: mset: 8 (over y, x, core), band: 4 (over z).
Axes of the slice: x: 2, y: 2, z: 4, core: 2. Of those that a mesh axis runs over, the one named last changes fastest.
Arguments:
- coeffs: bfloat16 [2, 704, 30720], P(None, 'band', 'mset'), may hold values from -6 to 6
- legendre: bfloat16 [320, 704, 512], P('mset', None, 'band'), may hold values from -0.3125 to 0.3125
- wavenumber: int32 [320], P('mset'), may hold values from 0 to 639, as said below
- band_rows: int32 [4], P('band'), may hold values from 16 to 128, as said below
Outputs:
- fourier: bfloat16 [96, 640, 512], P('mset', None, 'band')
The draws below stay inside these ranges and needn't reach their ends.
Inputs may be any that keep to these rules, and one draw needn't show every extreme that they name: All entries differ; pair q stands for wavenumbers wavenumber[q] and 1279 - wavenumber[q]. Both ends of the range occur. `band_rows`: entries 2 j and 2 j + 1 are equal (a band and its mirror image); some band holds 128.
All inputs are finite; a program needn't handle non-finite values.
Results may differ from the reference program's by a relative error of at most 0.0051.
Values may be sent and summed in bfloat16 or wider, within the bound.
No kernel may reach another device: no remote copies, remote signals or barrier semaphores. Data moves between devices by JAX's collectives and lax.ppermute only.
A program may use at most 128 MiB of HBM per device.

```python
import jax
import jax.numpy as jnp
from jax import lax

TRUNC = 1279
LAT_DEV = 128
ROWS = 704
PAIRS = 320
MTOTAL = 640
FIELDS2 = 96
BANDS = 4
NLAT = 512


def draw_wavenumber(key, part):
    half_count = (TRUNC + 1) // 2
    others = jax.random.permutation(key, half_count - 2).astype(jnp.int32) + 1
    chosen = jnp.concatenate([jnp.array([0, half_count - 1], dtype=jnp.int32), others[:PAIRS - 2]])
    order = jax.random.permutation(jax.random.fold_in(key, 7), PAIRS)
    return chosen[order]


def draw_band_rows(key, part):
    pair_bands = BANDS // 2
    band_counts = jax.random.randint(key, (pair_bands,), LAT_DEV // 8, LAT_DEV // 2 + 1, dtype=jnp.int32)
    fullest = jax.random.randint(jax.random.fold_in(key, 3), (), 0, pair_bands, dtype=jnp.int32)
    band_counts = jnp.where(jnp.arange(pair_bands, dtype=jnp.int32) == fullest, LAT_DEV, band_counts)
    return jnp.repeat(band_counts, 2).astype(jnp.int32)


def block_scale(rng, extent, shards, low, largest):
    gain, own = 1.0, jax.random.fold_in(rng, 6)
    for dim, parts in shards:
        steps = jnp.exp(jax.random.uniform(jax.random.fold_in(own, dim), (parts,), jnp.float32, low / len(shards), largest / len(shards)))
        gain = gain * jnp.repeat(steps, extent[dim] // parts).reshape([-1 if axis == dim else 1 for axis in range(len(extent))])
    return gain


def scatter_about(key, dims, width, reach, pieces=(), kind=jnp.bfloat16):
    values = width * jax.random.normal(key, dims, jnp.float32)
    if pieces:
        values = values * block_scale(key, dims, pieces, -0.22, 0.18)
    return jnp.clip(values, -reach, reach).astype(kind)


def setup_inputs(seed: int = 0) -> dict:
    key_of = jax.random.split(jax.random.key(seed), 5)
    return {
        "coeffs": scatter_about(key_of[0], (2, ROWS, PAIRS * FIELDS2), 1.0, 6.0, ((1, 4), (2, 8))),
        "legendre": scatter_about(key_of[1], (PAIRS, ROWS, NLAT), (ROWS // 2) ** -0.5, 0.3125, ((0, 8), (2, 4))),
        "wavenumber": draw_wavenumber(jax.random.fold_in(key_of[4], 71), 0),
        "band_rows": draw_band_rows(jax.random.fold_in(key_of[4], 71), 0),
    }


def reference(coeffs, legendre, wavenumber, band_rows):
    band_pairs = BANDS // 2
    lat_index = jnp.arange(NLAT, dtype=jnp.int32)
    valid_lat = (lat_index % LAT_DEV) < jnp.repeat(band_rows, LAT_DEV)
    row_index = jnp.arange(ROWS, dtype=jnp.int32)
    by_pair = jnp.transpose(coeffs.reshape(2, ROWS, PAIRS, FIELDS2), (2, 0, 1, 3))

    def one_pair(inputs):
        coeff_pair, legendre_pair, smaller = inputs
        shaped = legendre_pair.reshape(ROWS, band_pairs, 2, LAT_DEV)
        parity_sums = []
        for parity in range(2):
            first_count = jnp.maximum((TRUNC - smaller - parity) // 2 + 1, 0)
            second_count = jnp.maximum((smaller - parity) // 2 + 1, 0)
            in_first = row_index < first_count
            in_second = jnp.logical_and(jnp.logical_not(in_first), row_index < first_count + second_count)
            rows_here = coeff_pair[parity]
            nothing = jnp.zeros((), rows_here.dtype)
            stacked = jnp.concatenate([jnp.where(in_first[:, None], rows_here, nothing), jnp.where(in_second[:, None], rows_here, nothing)], axis=1)
            columns = shaped[:, :, parity, :].reshape(ROWS, band_pairs * LAT_DEV)
            part_sum = jnp.dot(stacked.T, columns, preferred_element_type=jnp.float32).astype(jnp.bfloat16)
            parity_sums.append(lax.optimization_barrier(part_sum).astype(jnp.float32))
        even_part = parity_sums[0].reshape(2 * FIELDS2, band_pairs, LAT_DEV)
        odd_part = parity_sums[1].reshape(2 * FIELDS2, band_pairs, LAT_DEV)
        hemispheres = jnp.stack([even_part + odd_part, even_part - odd_part], axis=2).reshape(2 * FIELDS2, NLAT)
        hemispheres = jnp.where(valid_lat[None, :], hemispheres, jnp.zeros((), hemispheres.dtype)).astype(jnp.bfloat16)
        return hemispheres.reshape(2, FIELDS2, NLAT)

    result = lax.map(one_pair, (by_pair, legendre, wavenumber))
    return jnp.transpose(result.reshape(MTOTAL, FIELDS2, NLAT), (1, 0, 2))
```

```python
import functools

import jax
import jax.numpy as jnp
from jax import lax
from jax.experimental import pallas as pl
from jax.experimental.pallas import tpu as pltpu
from jax.sharding import PartitionSpec as P

TRUNC = 1279
CHUNK = 8


def owner_limits(wavenumber, parity):
    first = jnp.maximum((TRUNC - wavenumber - parity) // 2 + 1, 0)
    second = jnp.maximum((wavenumber - parity) // 2 + 1, 0)
    return first, first + second


def sums_kernel(rows, fields, start, pairs, order, first, total, *refs):
    blocks, (legendre, out, gathered, flipped, values, sums, arrived) = refs[:-7], refs[-7:]
    _, depth, lats = legendre.shape
    copies = [
        pltpu.make_async_copy(legendre.at[start + pair], values.at[pair], arrived.at[pair]) for pair in range(pairs)
    ]
    for copy in copies:
        copy.start()
    if len(blocks) == 1:
        gathered[...] = blocks[0][...]
    else:
        for step, block in enumerate(blocks):
            offset = pl.multiple_of(order[step] * rows, 16)
            gathered[pl.ds(offset, rows), :] = block[...]
    flipped[...] = gathered[...].T
    row = lax.broadcasted_iota(jnp.int32, (depth, lats), 0)
    for pair in range(pairs):
        copies[pair].wait()
        here = values[pair].astype(jnp.float32)
        in_first = row < first[start + pair]
        in_any = row < total[start + pair]
        part_first = jnp.where(in_first, here, 0.0)
        part_second = jnp.where(in_any, here - part_first, 0.0)
        both = jnp.concatenate([part_first, part_second], axis=1).astype(jnp.bfloat16)
        product = jnp.dot(
            flipped[pair * fields : (pair + 1) * fields, :], both, preferred_element_type=jnp.float32
        )
        sums[:, 2 * pair, :] = product[:, :lats]
        sums[:, 2 * pair + 1, :] = product[:, lats:]
    out[...] = sums[...].astype(out.dtype)


def parity_sums(blocks, order, first, total, legendre, start, pairs, fields):
    rows, columns = blocks[0].shape
    _, depth, lats = legendre.shape
    vmem = pl.BlockSpec(memory_space=pltpu.VMEM)
    scalar = pl.BlockSpec(memory_space=pltpu.SMEM)
    return pl.pallas_call(
        functools.partial(sums_kernel, rows, fields, start, pairs),
        in_specs=[scalar] * 3 + [vmem] * len(blocks) + [pl.BlockSpec(memory_space=pltpu.HBM)],
        out_specs=vmem,
        scratch_shapes=[
            pltpu.VMEM((depth, columns), jnp.bfloat16),
            pltpu.VMEM((columns, depth), jnp.bfloat16),
            pltpu.VMEM((pairs, depth, lats), jnp.bfloat16),
            pltpu.VMEM((fields, 2 * pairs, lats), jnp.float32),
            pltpu.SemaphoreType.DMA((pairs,)),
        ],
        out_shape=jax.ShapeDtypeStruct((fields, 2 * pairs, lats), jnp.bfloat16),
        compiler_params=pltpu.CompilerParams(vmem_limit_bytes=56 * 2**20),
        cost_estimate=pl.CostEstimate(
            flops=4 * pairs * depth * fields * lats,
            bytes_accessed=2 * (depth * columns + pairs * depth * lats + 2 * pairs * fields * lats),
            transcendentals=0,
        ),
        name="parity_sums",
    )(order, first, total, *blocks, legendre)


def shards(coeffs, legendre, wavenumber, band_rows):
    bands = lax.axis_size("band")
    sets = lax.axis_size("mset")
    me = lax.axis_index("band")
    parity = me % 2
    pair_count, depth, lats = legendre.shape
    rows = coeffs.shape[1]
    fields = coeffs.shape[2] // pair_count
    first, total = owner_limits(wavenumber, parity)
    order = me ^ jnp.arange(bands, dtype=jnp.int32)
    valid_lat = jnp.arange(lats, dtype=jnp.int32) < band_rows[0]
    mine = lax.dynamic_index_in_dim(coeffs, parity, 0, keepdims=False)
    other = lax.dynamic_index_in_dim(coeffs, 1 - parity, 0, keepdims=False)
    chunks = pair_count // CHUNK
    steps = list(range(1, bands))

    def swap(value, step):
        return lax.ppermute(value, "band", [(band, band ^ step) for band in range(bands)])

    def columns_of(value, chunk):
        return value[:, chunk * CHUNK * fields : (chunk + 1) * CHUNK * fields]

    def combine(own, partner):
        own = own.astype(jnp.float32)
        partner = jnp.concatenate(partner).astype(jnp.float32)
        grid = jnp.where(parity == 0, own + partner, partner - own)
        return jnp.where(valid_lat, grid, 0.0).astype(jnp.bfloat16)

    def redistribute(grid):
        piece = lax.all_to_all(grid, "mset", split_axis=0, concat_axis=1, tiled=True)
        return piece.reshape(fields // sets, sets, 2 * CHUNK, lats)

    def start_sends(payloads):
        return [swap(payloads[step % 2], step) for step in steps]

    def payloads_of(chunk):
        return [columns_of(mine, chunk), columns_of(other, chunk)]

    blocks = start_sends(payloads_of(0))
    pieces = []
    halves = None
    for chunk in range(chunks):
        if chunk + 1 < chunks:
            blocks, later = lax.optimization_barrier((blocks, payloads_of(chunk + 1)))
            following = start_sends(later)
        if chunk >= 3:
            blocks, pieces[chunk - 3] = lax.optimization_barrier((blocks, pieces[chunk - 3]))
        blocks = [columns_of(mine, chunk)] + blocks
        if rows % 16:
            stacked = jnp.take(jnp.stack(blocks), me ^ jnp.arange(bands), axis=0)
            blocks = [stacked.reshape(bands * rows, -1)]
        own = parity_sums(blocks, order, first, total, legendre, chunk * CHUNK, CHUNK, fields)
        if halves is not None:
            own, halves = lax.optimization_barrier((own, halves))
            pieces.append(redistribute(combine(*halves)))
        middle = fields // 2
        halves = (own, [swap(own[:middle], 1), swap(own[middle:], 1)])
        blocks = following
    pieces.append(redistribute(combine(*halves)))
    return jnp.concatenate(pieces, axis=2).reshape(fields // sets, sets * 2 * pair_count, lats)


def solution(mesh):
    in_specs = (P(None, "band", "mset"), P("mset", None, "band"), P("mset"), P("band"))
    out_specs = P("mset", None, "band")
    return jax.shard_map(shards, mesh=mesh, in_specs=in_specs, out_specs=out_specs, check_vma=False)
```

```python
import functools

import jax
import jax.numpy as jnp
from jax import lax
from jax.experimental import pallas as pl
from jax.experimental.pallas import tpu as pltpu
from jax.sharding import PartitionSpec as P

TRUNC = 1279
CHUNKS = (8, 8, 8, 8, 4, 4)
GROUPS = ((0, 1), (2,), (3, 4, 5))


def owner_limits(wavenumber, parity):
    first = jnp.maximum((TRUNC - wavenumber - parity) // 2 + 1, 0)
    second = jnp.maximum((wavenumber - parity) // 2 + 1, 0)
    return first, first + second


def sums_kernel(rows, fields, start, order, first, total, *refs):
    blocks, (legendre, out, gathered, flipped, sums) = refs[:-5], refs[-5:]
    pairs, depth, lats = legendre.shape
    step = 0
    for part in blocks:
        for row in range(0, part.shape[0], rows):
            place = pl.ds(pl.multiple_of(order[step] * rows, 16), rows)
            gathered[place, :] = part[pl.ds(row, rows), :]
            step += 1
    flipped[...] = gathered[...].T
    row = lax.broadcasted_iota(jnp.int32, (depth, lats), 0)
    for pair in range(pairs):
        here = legendre[pair].astype(jnp.float32)
        in_first = row < first[start + pair]
        in_any = row < total[start + pair]
        part_first = jnp.where(in_first, here, 0.0)
        part_second = jnp.where(in_any, here - part_first, 0.0)
        both = jnp.concatenate([part_first, part_second], axis=1).astype(jnp.bfloat16)
        product = jnp.dot(
            flipped[pair * fields : (pair + 1) * fields, :], both, preferred_element_type=jnp.float32
        )
        sums[:, 2 * pair, :] = product[:, :lats]
        sums[:, 2 * pair + 1, :] = product[:, lats:]
    out[...] = sums[...].astype(out.dtype)


def parity_sums(blocks, rows, order, first, total, legendre, start, pairs, fields):
    columns = blocks[0].shape[1]
    _, depth, lats = legendre.shape
    legendre = legendre[start : start + pairs]
    vmem = pl.BlockSpec(memory_space=pltpu.VMEM)
    scalar = pl.BlockSpec(memory_space=pltpu.SMEM)
    return pl.pallas_call(
        functools.partial(sums_kernel, rows, fields, start),
        in_specs=[scalar] * 3 + [vmem] * (len(blocks) + 1),
        out_specs=vmem,
        scratch_shapes=[
            pltpu.VMEM((depth, columns), jnp.bfloat16),
            pltpu.VMEM((columns, depth), jnp.bfloat16),
            pltpu.VMEM((fields, 2 * pairs, lats), jnp.float32),
        ],
        out_shape=jax.ShapeDtypeStruct((fields, 2 * pairs, lats), jnp.bfloat16),
        compiler_params=pltpu.CompilerParams(vmem_limit_bytes=24 * 2**20),
        cost_estimate=pl.CostEstimate(flops=pairs * 10**11, bytes_accessed=pairs * 100 * 2**20, transcendentals=0),
        name="parity_sums",
    )(order, first, total, *blocks, legendre)


def shards(coeffs, legendre, wavenumber, band_rows):
    bands = lax.axis_size("band")
    sets = lax.axis_size("mset")
    me = lax.axis_index("band")
    parity = me % 2
    pair_count, depth, lats = legendre.shape
    rows = coeffs.shape[1]
    fields = coeffs.shape[2] // pair_count
    first, total = owner_limits(wavenumber, parity)
    order = (me if rows % 16 == 0 else 0) ^ jnp.arange(bands, dtype=jnp.int32)
    valid_lat = jnp.arange(lats, dtype=jnp.int32) < band_rows[0]
    assert sum(CHUNKS) == pair_count
    plan = [(sum(CHUNKS[:chunk]), pairs) for chunk, pairs in enumerate(CHUNKS)]
    def swap(value, step):
        return lax.ppermute(value, "band", [(band, band ^ step) for band in range(bands)])

    def payloads_of(chunk):
        start, pairs = plan[chunk]
        place, shape = (0, start * fields), (1, rows, pairs * fields)
        return [lax.dynamic_slice(coeffs, (which, *place), shape)[0] for which in (parity, 1 - parity)]

    def combine(own, partner):
        own, partner = own.astype(jnp.float32), partner.astype(jnp.float32)
        grid = jnp.where(parity == 0, own + partner, partner - own)
        return jnp.where(valid_lat, grid, 0.0).astype(jnp.bfloat16)

    def redistribute(grid):
        piece = lax.all_to_all(grid, "mset", split_axis=0, concat_axis=1, tiled=True)
        return piece.reshape(fields // sets, sets, -1, lats)

    def spread(mine, near):
        held = [mine, near]
        for bit in [2**power for power in range(1, bands.bit_length() - 1)]:
            held.append(swap(jnp.concatenate(held), bit))
        return held

    near, far, own_rows = {}, {}, {}

    def send_direct(payload):
        far[0] = [payload[0]] + [swap(payload[step % 2], step) for step in range(1, bands)]
        near[0] = far[0][1]

    def send_near(chunk):
        payload = payloads_of(chunk)
        if chunk >= 2:
            earlier = far[chunk - 3] if chunk >= 3 else near[chunk - 1]
            payload, earlier = lax.optimization_barrier((payload, earlier))
            if chunk >= 3:
                far[chunk - 3] = earlier
            else:
                near[chunk - 1] = earlier
        own_rows[chunk] = payload[0]
        near[chunk] = swap(payload[1], 1)

    def send_far(chunk):
        parts = [own_rows[chunk], near[chunk]]
        if chunk >= 2:
            parts, far[chunk - 2] = lax.optimization_barrier((parts, far[chunk - 2]))
        far[chunk] = spread(*parts)

    first_rows = payloads_of(0)
    coeffs, first_rows = lax.optimization_barrier((coeffs, first_rows))
    send_direct(first_rows)
    send_near(1)
    send_near(2)
    send_far(1)
    pieces, ready = [], []
    for chunk, (start, pairs) in enumerate(plan):
        if chunk + 2 < len(plan):
            send_far(chunk + 2)
        if 3 <= chunk + 3 < len(plan):
            send_near(chunk + 3)
        blocks = far[chunk]
        if rows % 16:
            stacked = jnp.concatenate(blocks).reshape(bands, rows, -1)
            blocks = [jnp.take(stacked, me ^ jnp.arange(bands), axis=0).reshape(bands * rows, -1)]
        own = parity_sums(
            blocks, rows if rows % 16 == 0 else depth, order, first, total, legendre, start, pairs, fields
        )
        ready.append((own, swap(own, 1)))
        if chunk == GROUPS[len(pieces)][-1]:
            ready, pieces[-1:] = lax.optimization_barrier((ready, pieces[-1:]))
            pieces.append(redistribute(jnp.concatenate([combine(*part) for part in ready], axis=1)))
            ready = []
    return jnp.concatenate(pieces, axis=2).reshape(fields // sets, sets * 2 * pair_count, lats)


def solution(mesh):
    in_specs = (P(None, "band", "mset"), P("mset", None, "band"), P("mset"), P("band"))
    out_specs = P("mset", None, "band")
    return jax.shard_map(shards, mesh=mesh, in_specs=in_specs, out_specs=out_specs, check_vma=False)
```

```python
import functools

import jax
import jax.numpy as jnp
from jax import lax
from jax.experimental import pallas as pl
from jax.experimental.pallas import tpu as pltpu
from jax.sharding import PartitionSpec as P

TRUNC = 1279
VMEM = 24 * 2**20
CHUNKS = (8, 8, 8, 8, 4, 4)
GROUPS = ((0, 1), (2,), (3, 4, 5))


def owner_limits(wavenumber, parity):
    first = jnp.maximum((TRUNC - wavenumber - parity) // 2 + 1, 0)
    second = jnp.maximum((wavenumber - parity) // 2 + 1, 0)
    return first, first + second


def sums_kernel(rows, fields, start, order, first, total, *refs):
    blocks, (legendre, out, gathered, flipped, sums) = refs[:-5], refs[-5:]
    pairs, depth, lats = legendre.shape
    step = 0
    for part in blocks:
        for row in range(0, part.shape[0], rows):
            place = pl.ds(pl.multiple_of(order[step] * rows, 16), rows)
            gathered[place, :] = part[pl.ds(row, rows), :]
            step += 1
    flipped[...] = gathered[...].T
    row = lax.broadcasted_iota(jnp.int32, (depth, lats), 0)
    for pair in range(pairs):
        here = legendre[pair].astype(jnp.float32)
        in_first = row < first[start + pair]
        in_any = row < total[start + pair]
        part_first = jnp.where(in_first, here, 0.0)
        part_second = jnp.where(in_any, here - part_first, 0.0)
        both = jnp.concatenate([part_first, part_second], axis=1).astype(jnp.bfloat16)
        product = jnp.dot(
            flipped[pair * fields : (pair + 1) * fields, :], both, preferred_element_type=jnp.float32
        )
        sums[:, 2 * pair, :] = product[:, :lats]
        sums[:, 2 * pair + 1, :] = product[:, lats:]
    out[...] = sums[...].astype(out.dtype)


def parity_sums(blocks, rows, order, first, total, legendre, start, pairs, fields):
    columns = blocks[0].shape[1]
    _, depth, lats = legendre.shape
    legendre = legendre[start : start + pairs]
    vmem = pl.BlockSpec(memory_space=pltpu.VMEM)
    scalar = pl.BlockSpec(memory_space=pltpu.SMEM)
    return pl.pallas_call(
        functools.partial(sums_kernel, rows, fields, start),
        in_specs=[scalar] * 3 + [vmem] * (len(blocks) + 1),
        out_specs=vmem,
        scratch_shapes=[
            pltpu.VMEM((depth, columns), jnp.bfloat16),
            pltpu.VMEM((columns, depth), jnp.bfloat16),
            pltpu.VMEM((fields, 2 * pairs, lats), jnp.float32),
        ],
        out_shape=jax.ShapeDtypeStruct((fields, 2 * pairs, lats), jnp.bfloat16),
        compiler_params=pltpu.CompilerParams(vmem_limit_bytes=VMEM),
        cost_estimate=pl.CostEstimate(flops=pairs * 10**11, bytes_accessed=pairs * 100 * 2**20, transcendentals=0),
        name="parity_sums",
    )(order, first, total, *blocks, legendre)


def combine_kernel(count, parity, lat_count, *refs):
    out = refs[-1]
    slot = 0
    for own, partner in zip(refs[:count], refs[count:-1]):
        wide, other = own[...].astype(jnp.float32), partner[...].astype(jnp.float32)
        grid = other + jnp.where(parity[0] == 0, 1.0, -1.0) * wide
        lat = lax.broadcasted_iota(jnp.int32, grid.shape, 2)
        out[:, slot : slot + own.shape[1], :] = jnp.where(lat < lat_count[0], grid, 0.0).astype(out.dtype)
        slot += own.shape[1]


def combine(halves, parity, lat_count):
    owns, partners = zip(*halves)
    fields, _, lats = owns[0].shape
    vmem = pl.BlockSpec(memory_space=pltpu.VMEM)
    scalar = pl.BlockSpec(memory_space=pltpu.SMEM)
    return pl.pallas_call(
        functools.partial(combine_kernel, len(owns)),
        in_specs=[scalar] * 2 + [vmem] * (2 * len(owns)),
        out_specs=vmem,
        out_shape=jax.ShapeDtypeStruct((fields, sum(own.shape[1] for own in owns), lats), jnp.bfloat16),
        compiler_params=pltpu.CompilerParams(vmem_limit_bytes=VMEM),
        name="combine",
    )(parity.reshape(1), lat_count, *owns, *partners)


def place_kernel(first_slot, slots, count, *refs):
    pieces, out, done = refs[:count], refs[-2], refs[-1]
    copies = []
    for piece in pieces:
        sets, _, width, _ = piece.shape
        for group in range(sets):
            target = out.at[:, pl.ds(group * slots + first_slot, width), :]
            copies.append(pltpu.make_async_copy(piece.at[group], target, done.at[len(copies)]))
        first_slot += width
    for copy in copies:
        copy.start()
    for copy in copies:
        copy.wait()


def place(pieces, first_slot, slots, out):
    sets, fields, _, lats = pieces[0].shape
    vmem = pl.BlockSpec(memory_space=pltpu.VMEM)
    hbm = pl.BlockSpec(memory_space=pltpu.HBM)
    held = [] if out is None else [out]
    return pl.pallas_call(
        functools.partial(place_kernel, first_slot, slots, len(pieces)),
        in_specs=[vmem] * len(pieces) + [hbm] * len(held),
        out_specs=hbm,
        scratch_shapes=[pltpu.SemaphoreType.DMA((len(pieces) * sets,))],
        out_shape=jax.ShapeDtypeStruct((fields, sets * slots, lats), jnp.bfloat16),
        input_output_aliases={len(pieces): 0} if held else {},
        compiler_params=pltpu.CompilerParams(vmem_limit_bytes=VMEM),
        name="place",
    )(*pieces, *held)


def shards(coeffs, legendre, wavenumber, band_rows):
    bands = lax.axis_size("band")
    sets = lax.axis_size("mset")
    me = lax.axis_index("band")
    parity = me % 2
    pair_count, depth, lats = legendre.shape
    rows = coeffs.shape[1]
    fields = coeffs.shape[2] // pair_count
    first, total = owner_limits(wavenumber, parity)
    order = (me if rows % 16 == 0 else 0) ^ jnp.arange(bands, dtype=jnp.int32)
    assert sum(CHUNKS) == pair_count
    plan = [(sum(CHUNKS[:chunk]), pairs) for chunk, pairs in enumerate(CHUNKS)]
    def swap(value, step):
        return lax.ppermute(value, "band", [(band, band ^ step) for band in range(bands)])

    def payloads_of(chunk):
        start, pairs = plan[chunk]
        place, shape = (0, start * fields), (1, rows, pairs * fields)
        return [lax.dynamic_slice(coeffs, (which, *place), shape)[0] for which in (parity, 1 - parity)]

    def redistribute(grid):
        return lax.all_to_all(grid.reshape(sets, fields // sets, -1, lats), "mset", 0, 0)

    def spread(mine, near):
        held = [mine, near]
        for bit in [2**power for power in range(1, bands.bit_length() - 1)]:
            held.append(swap(jnp.concatenate(held), bit))
        return held

    near, far, own_rows = {}, {}, {}

    def send_direct(payload):
        far[0] = [payload[0]] + [swap(payload[step % 2], step) for step in range(1, bands)]
        near[0] = far[0][1]

    def send_near(chunk):
        payload = payloads_of(chunk)
        if chunk >= 2:
            earlier = far[chunk - 3] if chunk >= 3 else near[chunk - 1]
            payload, earlier = lax.optimization_barrier((payload, earlier))
            if chunk >= 3:
                far[chunk - 3] = earlier
            else:
                near[chunk - 1] = earlier
        own_rows[chunk] = payload[0]
        near[chunk] = swap(payload[1], 1)

    def send_far(chunk, after=None):
        parts = [own_rows[chunk], near[chunk]]
        if after is not None:
            parts, after = lax.optimization_barrier((parts, after))
        far[chunk] = spread(*parts)
        return after

    first_rows = payloads_of(0)
    coeffs, first_rows = lax.optimization_barrier((coeffs, first_rows))
    send_direct(first_rows)
    send_near(1)
    send_near(2)
    send_far(1)
    pieces, ready = [], []
    for chunk, (start, pairs) in enumerate(plan):
        if 3 <= chunk + 3 < len(plan):
            send_near(chunk + 3)
        if chunk < 1:
            far[chunk], near[chunk + 2] = lax.optimization_barrier((far[chunk], near[chunk + 2]))
        blocks = far[chunk]
        if rows % 16:
            stacked = jnp.concatenate(blocks).reshape(bands, rows, -1)
            blocks = [jnp.take(stacked, me ^ jnp.arange(bands), axis=0).reshape(bands * rows, -1)]
        own = parity_sums(
            blocks, rows if rows % 16 == 0 else depth, order, first, total, legendre, start, pairs, fields
        )
        if chunk + 2 < len(plan):
            own = send_far(chunk + 2, own)
        ready.append((own, swap(own, 1)))
        if chunk == GROUPS[len(pieces)][-1]:
            ready, pieces[-1:] = lax.optimization_barrier((ready, pieces[-1:]))
            pieces.append(redistribute(combine(ready, parity, band_rows)))
            ready = []
    ahead = place(pieces[:-1], 0, 2 * pair_count, None)
    return place(pieces[-1:], sum(piece.shape[2] for piece in pieces[:-1]), 2 * pair_count, ahead)


def solution(mesh):
    in_specs = (P(None, "band", "mset"), P("mset", None, "band"), P("mset"), P("band"))
    out_specs = P("mset", None, "band")
    return jax.shard_map(shards, mesh=mesh, in_specs=in_specs, out_specs=out_specs, check_vma=False)
```

```python
import functools

import jax
import jax.numpy as jnp
from jax import lax
from jax.experimental import pallas as pl
from jax.experimental.pallas import tpu as pltpu
from jax.sharding import PartitionSpec as P

TRUNC = 1279
VMEM = 24 * 2**20
CHUNKS = (8, 8, 8, 8, 4, 4)
GROUPS = ((0, 1), (2, 3), (4, 5))


def owner_limits(wavenumber, parity):
    first = jnp.maximum((TRUNC - wavenumber - parity) // 2 + 1, 0)
    second = jnp.maximum((wavenumber - parity) // 2 + 1, 0)
    return first, first + second


def sums_kernel(rows, fields, start, order, first, total, *refs):
    blocks, (legendre, out, gathered, flipped, sums) = refs[:-5], refs[-5:]
    pairs, depth, lats = legendre.shape
    step = 0
    for part in blocks:
        for row in range(0, part.shape[0], rows):
            place = pl.ds(pl.multiple_of(order[step] * rows, 16), rows)
            gathered[place, :] = part[pl.ds(row, rows), :]
            step += 1
    flipped[...] = gathered[...].T
    row = lax.broadcasted_iota(jnp.int32, (depth, lats), 0)
    for pair in range(pairs):
        here = legendre[pair].astype(jnp.float32)
        in_first = row < first[start + pair]
        in_any = row < total[start + pair]
        part_first = jnp.where(in_first, here, 0.0)
        part_second = jnp.where(in_any, here - part_first, 0.0)
        both = jnp.concatenate([part_first, part_second], axis=1).astype(jnp.bfloat16)
        product = jnp.dot(
            flipped[pair * fields : (pair + 1) * fields, :], both, preferred_element_type=jnp.float32
        )
        sums[:, 2 * pair, :] = product[:, :lats]
        sums[:, 2 * pair + 1, :] = product[:, lats:]
    out[...] = sums[...].astype(out.dtype)


def parity_sums(blocks, rows, order, first, total, legendre, start, pairs, fields):
    columns = blocks[0].shape[1]
    _, depth, lats = legendre.shape
    legendre = legendre[start : start + pairs]
    vmem = pl.BlockSpec(memory_space=pltpu.VMEM)
    scalar = pl.BlockSpec(memory_space=pltpu.SMEM)
    return pl.pallas_call(
        functools.partial(sums_kernel, rows, fields, start),
        in_specs=[scalar] * 3 + [vmem] * (len(blocks) + 1),
        out_specs=vmem,
        scratch_shapes=[
            pltpu.VMEM((depth, columns), jnp.bfloat16),
            pltpu.VMEM((columns, depth), jnp.bfloat16),
            pltpu.VMEM((fields, 2 * pairs, lats), jnp.float32),
        ],
        out_shape=jax.ShapeDtypeStruct((fields, 2 * pairs, lats), jnp.bfloat16),
        compiler_params=pltpu.CompilerParams(vmem_limit_bytes=VMEM),
        cost_estimate=pl.CostEstimate(flops=pairs * 10**11, bytes_accessed=pairs * 100 * 2**20, transcendentals=0),
        name="parity_sums",
    )(order, first, total, *blocks, legendre)


def finish_kernel(first_slot, slots, count, parity, lat_count, *refs):
    owns, partners, (out, result, done) = refs[:count], refs[count : 2 * count], refs[-3:]
    sets, _, width, _ = result.shape
    sign = jnp.where(parity[0] == 0, 1.0, -1.0)
    copies = []
    for group in range(sets):
        slot = 0
        for own, partner in zip(owns, partners):
            grid = partner[group].astype(jnp.float32) + sign * own[group].astype(jnp.float32)
            lat = lax.broadcasted_iota(jnp.int32, grid.shape, 2)
            grid = jnp.where(lat < lat_count[0], grid, 0.0)
            result[group, :, slot : slot + own.shape[2], :] = grid.astype(result.dtype)
            slot += own.shape[2]
        target = out.at[:, pl.ds(group * slots + first_slot, width), :]
        copies.append(pltpu.make_async_copy(result.at[group], target, done.at[group]))
        copies[-1].start()
    for copy in copies:
        copy.wait()


def finish(halves, parity, lat_count, first_slot, slots, out):
    owns, partners = zip(*halves)
    sets, fields, _, lats = owns[0].shape
    width = sum(own.shape[2] for own in owns)
    vmem = pl.BlockSpec(memory_space=pltpu.VMEM)
    hbm = pl.BlockSpec(memory_space=pltpu.HBM)
    scalar = pl.BlockSpec(memory_space=pltpu.SMEM)
    held = [] if out is None else [out]
    return pl.pallas_call(
        functools.partial(finish_kernel, first_slot, slots, len(owns)),
        in_specs=[scalar] * 2 + [vmem] * (2 * len(owns)) + [hbm] * len(held),
        out_specs=hbm,
        scratch_shapes=[
            pltpu.VMEM((sets, fields, width, lats), jnp.bfloat16),
            pltpu.SemaphoreType.DMA((sets,)),
        ],
        out_shape=jax.ShapeDtypeStruct((fields, sets * slots, lats), jnp.bfloat16),
        input_output_aliases={2 + 2 * len(owns): 0} if held else {},
        compiler_params=pltpu.CompilerParams(vmem_limit_bytes=VMEM),
        name="finish",
    )(parity.reshape(1), lat_count, *owns, *partners, *held)


def shards(coeffs, legendre, wavenumber, band_rows):
    bands = lax.axis_size("band")
    sets = lax.axis_size("mset")
    me = lax.axis_index("band")
    parity = me % 2
    pair_count, depth, lats = legendre.shape
    rows = coeffs.shape[1]
    fields = coeffs.shape[2] // pair_count
    first, total = owner_limits(wavenumber, parity)
    order = (me if rows % 16 == 0 else 0) ^ jnp.arange(bands, dtype=jnp.int32)
    assert sum(CHUNKS) == pair_count
    plan = [(sum(CHUNKS[:chunk]), pairs) for chunk, pairs in enumerate(CHUNKS)]
    def swap(value, step):
        return lax.ppermute(value, "band", [(band, band ^ step) for band in range(bands)])

    def payloads_of(chunk):
        start, pairs = plan[chunk]
        place, shape = (0, start * fields), (1, rows, pairs * fields)
        return [lax.dynamic_slice(coeffs, (which, *place), shape)[0] for which in (parity, 1 - parity)]

    def redistribute(grid):
        return lax.all_to_all(grid.reshape(sets, fields // sets, -1, lats), "mset", 0, 0)

    def spread(mine, near):
        held = [mine, near]
        for bit in [2**power for power in range(1, bands.bit_length() - 1)]:
            held.append(swap(jnp.concatenate(held), bit))
        return held

    near, far, own_rows = {}, {}, {}

    def send_direct(payload):
        far[0] = [payload[0]] + [swap(payload[step % 2], step) for step in range(1, bands)]
        near[0] = far[0][1]

    def send_near(chunk):
        payload = payloads_of(chunk)
        if chunk >= 2:
            earlier = far[chunk - 3] if chunk >= 3 else near[chunk - 1]
            payload, earlier = lax.optimization_barrier((payload, earlier))
            if chunk >= 3:
                far[chunk - 3] = earlier
            else:
                near[chunk - 1] = earlier
        own_rows[chunk] = payload[0]
        near[chunk] = swap(payload[1], 1)

    def send_far(chunk, after=None):
        parts = [own_rows[chunk], near[chunk]]
        if after is not None:
            parts, after = lax.optimization_barrier((parts, after))
        far[chunk] = spread(*parts)
        return after

    first_rows = payloads_of(0)
    coeffs, first_rows = lax.optimization_barrier((coeffs, first_rows))
    send_direct(first_rows)
    send_near(1)
    send_near(2)
    send_far(1)
    out, written, ready = None, 0, []
    for chunk, (start, pairs) in enumerate(plan):
        if 3 <= chunk + 3 < len(plan):
            send_near(chunk + 3)
        if chunk < 1:
            far[chunk], near[chunk + 2] = lax.optimization_barrier((far[chunk], near[chunk + 2]))
        blocks = far[chunk]
        if rows % 16:
            stacked = jnp.concatenate(blocks).reshape(bands, rows, -1)
            blocks = [jnp.take(stacked, me ^ jnp.arange(bands), axis=0).reshape(bands * rows, -1)]
        own = parity_sums(
            blocks, rows if rows % 16 == 0 else depth, order, first, total, legendre, start, pairs, fields
        )
        if chunk + 2 < len(plan):
            own = send_far(chunk + 2, own)
        piece = redistribute(own)
        ready.append((piece, swap(piece, 1)))
        if chunk == GROUPS[written][-1]:
            first_slot = 2 * plan[GROUPS[written][0]][0]
            out = finish(ready, parity, band_rows, first_slot, 2 * pair_count, out)
            written, ready = written + 1, []
    return out


def solution(mesh):
    in_specs = (P(None, "band", "mset"), P("mset", None, "band"), P("mset"), P("band"))
    out_specs = P("mset", None, "band")
    return jax.shard_map(shards, mesh=mesh, in_specs=in_specs, out_specs=out_specs, check_vma=False)
```

```python
import functools

import jax
import jax.numpy as jnp
from jax import lax
from jax.experimental import pallas as pl
from jax.experimental.pallas import tpu as pltpu
from jax.sharding import PartitionSpec as P

TRUNC = 1279
VMEM = 24 * 2**20
CHUNKS = (8, 8, 8, 8, 4, 4)
GROUPS = ((0, 1), (2, 3), (4, 5))


def owner_limits(wavenumber, parity):
    first = jnp.maximum((TRUNC - wavenumber - parity) // 2 + 1, 0)
    second = jnp.maximum((wavenumber - parity) // 2 + 1, 0)
    return first, first + second


def sums_kernel(rows, fields, start, order, first, total, *refs):
    blocks, (legendre, out, gathered, flipped, sums) = refs[:-5], refs[-5:]
    pairs, depth, lats = legendre.shape
    step = 0
    for part in blocks:
        for row in range(0, part.shape[0], rows):
            place = pl.ds(pl.multiple_of(order[step] * rows, 16), rows)
            gathered[place, :] = part[pl.ds(row, rows), :]
            step += 1
    flipped[...] = gathered[...].T
    row = lax.broadcasted_iota(jnp.int32, (depth, lats), 0)
    for pair in range(pairs):
        here = legendre[pair].astype(jnp.float32)
        in_first = row < first[start + pair]
        in_any = row < total[start + pair]
        part_first = jnp.where(in_first, here, 0.0)
        part_second = jnp.where(in_any, here - part_first, 0.0)
        both = jnp.concatenate([part_first, part_second], axis=1).astype(jnp.bfloat16)
        product = jnp.dot(
            flipped[pair * fields : (pair + 1) * fields, :], both, preferred_element_type=jnp.float32
        )
        sums[:, 2 * pair, :] = product[:, :lats]
        sums[:, 2 * pair + 1, :] = product[:, lats:]
    out[...] = sums[...].astype(out.dtype)


def parity_sums(blocks, rows, order, first, total, legendre, start, pairs, fields):
    columns = blocks[0].shape[1]
    _, depth, lats = legendre.shape
    legendre = legendre[start : start + pairs]
    vmem = pl.BlockSpec(memory_space=pltpu.VMEM)
    scalar = pl.BlockSpec(memory_space=pltpu.SMEM)
    return pl.pallas_call(
        functools.partial(sums_kernel, rows, fields, start),
        in_specs=[scalar] * 3 + [vmem] * (len(blocks) + 1),
        out_specs=vmem,
        scratch_shapes=[
            pltpu.VMEM((depth, columns), jnp.bfloat16),
            pltpu.VMEM((columns, depth), jnp.bfloat16),
            pltpu.VMEM((fields, 2 * pairs, lats), jnp.float32),
        ],
        out_shape=jax.ShapeDtypeStruct((fields, 2 * pairs, lats), jnp.bfloat16),
        compiler_params=pltpu.CompilerParams(vmem_limit_bytes=VMEM),
        cost_estimate=pl.CostEstimate(flops=pairs * 10**11, bytes_accessed=pairs * 100 * 2**20, transcendentals=0),
        name="parity_sums",
    )(order, first, total, *blocks, legendre)


def finish_kernel(first_slot, slots, count, parity, lat_count, *refs):
    owns, partners, (out, result, done) = refs[:count], refs[count : 2 * count], refs[-3:]
    sets, _, width, _ = result.shape
    sign = jnp.where(parity[0] == 0, 1.0, -1.0)
    copies = []
    for group in range(sets):
        slot = 0
        for own, partner in zip(owns, partners):
            grid = partner[group].astype(jnp.float32) + sign * own[group].astype(jnp.float32)
            lat = lax.broadcasted_iota(jnp.int32, grid.shape, 2)
            grid = jnp.where(lat < lat_count[0], grid, 0.0)
            result[group, :, slot : slot + own.shape[2], :] = grid.astype(result.dtype)
            slot += own.shape[2]
        target = out.at[:, pl.ds(group * slots + first_slot, width), :]
        copies.append(pltpu.make_async_copy(result.at[group], target, done.at[group]))
        copies[-1].start()
    for copy in copies:
        copy.wait()


def finish(halves, parity, lat_count, first_slot, slots, out):
    owns, partners = zip(*halves)
    sets, fields, _, lats = owns[0].shape
    width = sum(own.shape[2] for own in owns)
    vmem = pl.BlockSpec(memory_space=pltpu.VMEM)
    hbm = pl.BlockSpec(memory_space=pltpu.HBM)
    scalar = pl.BlockSpec(memory_space=pltpu.SMEM)
    held = [] if out is None else [out]
    return pl.pallas_call(
        functools.partial(finish_kernel, first_slot, slots, len(owns)),
        in_specs=[scalar] * 2 + [vmem] * (2 * len(owns)) + [hbm] * len(held),
        out_specs=hbm,
        scratch_shapes=[
            pltpu.VMEM((sets, fields, width, lats), jnp.bfloat16),
            pltpu.SemaphoreType.DMA((sets,)),
        ],
        out_shape=jax.ShapeDtypeStruct((fields, sets * slots, lats), jnp.bfloat16),
        input_output_aliases={2 + 2 * len(owns): 0} if held else {},
        compiler_params=pltpu.CompilerParams(vmem_limit_bytes=VMEM),
        name="finish",
    )(parity.reshape(1), lat_count, *owns, *partners, *held)


def shards(coeffs, legendre, wavenumber, band_rows):
    bands = lax.axis_size("band")
    sets = lax.axis_size("mset")
    me = lax.axis_index("band")
    parity = me % 2
    pair_count, depth, lats = legendre.shape
    rows = coeffs.shape[1]
    fields = coeffs.shape[2] // pair_count
    first, total = owner_limits(wavenumber, parity)
    order = (me if rows % 16 == 0 else 0) ^ jnp.arange(bands, dtype=jnp.int32)
    assert sum(CHUNKS) == pair_count
    plan = [(sum(CHUNKS[:chunk]), pairs) for chunk, pairs in enumerate(CHUNKS)]
    def swap(value, step):
        return lax.ppermute(value, "band", [(band, band ^ step) for band in range(bands)])

    def payloads_of(chunk):
        start, pairs = plan[chunk]
        place, shape = (0, start * fields), (1, rows, pairs * fields)
        return [lax.dynamic_slice(coeffs, (which, *place), shape)[0] for which in (parity, 1 - parity)]

    def redistribute(grid):
        return lax.all_to_all(grid.reshape(sets, fields // sets, -1, lats), "mset", 0, 0)

    def spread(mine, near):
        held = [mine, near]
        for bit in [2**power for power in range(1, bands.bit_length() - 1)]:
            held.append(swap(jnp.concatenate(held), bit))
        return held

    near, far, own_rows = {}, {}, {}

    def send_direct(payload):
        far[0] = [payload[0]] + [swap(payload[step % 2], step) for step in range(1, bands)]
        near[0] = far[0][1]

    def send_near(chunk):
        payload = payloads_of(chunk)
        if chunk >= 2:
            earlier = far[chunk - 3] if chunk >= 3 else near[chunk - 1]
            payload, earlier = lax.optimization_barrier((payload, earlier))
            if chunk >= 3:
                far[chunk - 3] = earlier
            else:
                near[chunk - 1] = earlier
        own_rows[chunk] = payload[0]
        near[chunk] = swap(payload[1], 1)

    def send_far(chunk, after=None):
        parts = [own_rows[chunk], near[chunk]]
        if after is not None:
            parts, after = lax.optimization_barrier((parts, after))
        far[chunk] = spread(*parts)
        return after

    first_rows = payloads_of(0)
    coeffs, first_rows = lax.optimization_barrier((coeffs, first_rows))
    send_direct(first_rows)
    send_near(1)
    send_near(2)
    send_far(1)
    out, written, sums = None, 0, []

    def write():
        nonlocal out, written
        first_slot = 2 * plan[GROUPS[written][0]][0]
        parts = [sums[chunk] for chunk in GROUPS[written]]
        out = finish(parts, parity, band_rows, first_slot, 2 * pair_count, out)
        written += 1

    for chunk, (start, pairs) in enumerate(plan):
        if 3 <= chunk + 3 < len(plan):
            send_near(chunk + 3)
        if chunk < 1:
            far[chunk], near[chunk + 2] = lax.optimization_barrier((far[chunk], near[chunk + 2]))
        if 0 < chunk < len(plan) - 0:
            far[chunk], piece = lax.optimization_barrier((far[chunk], piece))
            sums.append((piece, swap(piece, 1)))
        elif chunk > 0:
            sums.append((piece, swap(piece, 1)))
        if 2 <= chunk < len(plan) - 1:
            far[chunk], sums[chunk - 2] = lax.optimization_barrier((far[chunk], sums[chunk - 2]))
        blocks = far[chunk]
        if rows % 16:
            stacked = jnp.concatenate(blocks).reshape(bands, rows, -1)
            blocks = [jnp.take(stacked, me ^ jnp.arange(bands), axis=0).reshape(bands * rows, -1)]
        own = parity_sums(
            blocks, rows if rows % 16 == 0 else depth, order, first, total, legendre, start, pairs, fields
        )
        if chunk + 2 < len(plan):
            own = send_far(chunk + 2, own)
        piece = redistribute(own)
    sums.append((piece, swap(piece, 1)))
    while written < len(GROUPS):
        write()
    return out


def solution(mesh):
    in_specs = (P(None, "band", "mset"), P("mset", None, "band"), P("mset"), P("band"))
    out_specs = P("mset", None, "band")
    return jax.shard_map(shards, mesh=mesh, in_specs=in_specs, out_specs=out_specs, check_vma=False)
```

```python
import functools

import jax
import jax.numpy as jnp
from jax import lax
from jax.experimental import pallas as pl
from jax.experimental.pallas import tpu as pltpu
from jax.sharding import PartitionSpec as P

TRUNC = 1279
VMEM = 24 * 2**20
CHUNKS = (8, 8, 8, 8, 4, 4)
MIRRORED = {2: 0, 3: 1, 5: 2}
GROUPS = ((0, 1), (2, 3), (4, 5))


def owner_limits(wavenumber, parity):
    first = jnp.maximum((TRUNC - wavenumber - parity) // 2 + 1, 0)
    second = jnp.maximum((wavenumber - parity) // 2 + 1, 0)
    return first, first + second


def sums_kernel(rows, fields, start, order, first, total, *refs):
    blocks, (legendre, out, gathered, flipped, sums) = refs[:-5], refs[-5:]
    pairs, depth, lats = legendre.shape
    step = 0
    for part in blocks:
        for row in range(0, part.shape[0], rows):
            place = pl.ds(pl.multiple_of(order[step] * rows, 16), rows)
            gathered[place, :] = part[pl.ds(row, rows), :]
            step += 1
    flipped[...] = gathered[...].T
    row = lax.broadcasted_iota(jnp.int32, (depth, lats), 0)
    for pair in range(pairs):
        here = legendre[pair].astype(jnp.float32)
        in_first = row < first[start + pair]
        in_any = row < total[start + pair]
        part_first = jnp.where(in_first, here, 0.0)
        part_second = jnp.where(in_any, here - part_first, 0.0)
        both = jnp.concatenate([part_first, part_second], axis=1).astype(jnp.bfloat16)
        product = jnp.dot(
            flipped[pair * fields : (pair + 1) * fields, :], both, preferred_element_type=jnp.float32
        )
        sums[:, 2 * pair, :] = product[:, :lats]
        sums[:, 2 * pair + 1, :] = product[:, lats:]
    out[...] = sums[...].astype(out.dtype)


def parity_sums(blocks, rows, order, first, total, legendre, start, pairs, fields):
    columns = blocks[0].shape[1]
    _, depth, lats = legendre.shape
    legendre = legendre[start : start + pairs]
    vmem = pl.BlockSpec(memory_space=pltpu.VMEM)
    scalar = pl.BlockSpec(memory_space=pltpu.SMEM)
    return pl.pallas_call(
        functools.partial(sums_kernel, rows, fields, start),
        in_specs=[scalar] * 3 + [vmem] * (len(blocks) + 1),
        out_specs=vmem,
        scratch_shapes=[
            pltpu.VMEM((depth, columns), jnp.bfloat16),
            pltpu.VMEM((columns, depth), jnp.bfloat16),
            pltpu.VMEM((fields, 2 * pairs, lats), jnp.float32),
        ],
        out_shape=jax.ShapeDtypeStruct((fields, 2 * pairs, lats), jnp.bfloat16),
        compiler_params=pltpu.CompilerParams(vmem_limit_bytes=VMEM),
        cost_estimate=pl.CostEstimate(flops=pairs * 10**11, bytes_accessed=pairs * 100 * 2**20, transcendentals=0),
        name="parity_sums",
    )(order, first, total, *blocks, legendre)


def finish_kernel(first_slot, slots, count, parity, lat_count, *refs):
    owns, partners, (out, result, done) = refs[:count], refs[count : 2 * count], refs[-3:]
    sets, _, width, _ = result.shape
    sign = jnp.where(parity[0] == 0, 1.0, -1.0)
    copies = []
    for group in range(sets):
        slot = 0
        for own, partner in zip(owns, partners):
            grid = partner[group].astype(jnp.float32) + sign * own[group].astype(jnp.float32)
            lat = lax.broadcasted_iota(jnp.int32, grid.shape, 2)
            grid = jnp.where(lat < lat_count[0], grid, 0.0)
            result[group, :, slot : slot + own.shape[2], :] = grid.astype(result.dtype)
            slot += own.shape[2]
        target = out.at[:, pl.ds(group * slots + first_slot, width), :]
        copies.append(pltpu.make_async_copy(result.at[group], target, done.at[group]))
        copies[-1].start()
    for copy in copies:
        copy.wait()


def finish(halves, parity, lat_count, first_slot, slots, out):
    owns, partners = zip(*halves)
    sets, fields, _, lats = owns[0].shape
    width = sum(own.shape[2] for own in owns)
    vmem = pl.BlockSpec(memory_space=pltpu.VMEM)
    hbm = pl.BlockSpec(memory_space=pltpu.HBM)
    scalar = pl.BlockSpec(memory_space=pltpu.SMEM)
    held = [] if out is None else [out]
    return pl.pallas_call(
        functools.partial(finish_kernel, first_slot, slots, len(owns)),
        in_specs=[scalar] * 2 + [vmem] * (2 * len(owns)) + [hbm] * len(held),
        out_specs=hbm,
        scratch_shapes=[
            pltpu.VMEM((sets, fields, width, lats), jnp.bfloat16),
            pltpu.SemaphoreType.DMA((sets,)),
        ],
        out_shape=jax.ShapeDtypeStruct((fields, sets * slots, lats), jnp.bfloat16),
        input_output_aliases={2 + 2 * len(owns): 0} if held else {},
        compiler_params=pltpu.CompilerParams(vmem_limit_bytes=VMEM),
        name="finish",
    )(parity.reshape(1), lat_count, *owns, *partners, *held)


def shards(coeffs, legendre, wavenumber, band_rows):
    bands = lax.axis_size("band")
    sets = lax.axis_size("mset")
    me = lax.axis_index("band")
    parity = me % 2
    pair_count, depth, lats = legendre.shape
    rows = coeffs.shape[1]
    fields = coeffs.shape[2] // pair_count
    first, total = owner_limits(wavenumber, parity)
    order = (me if rows % 16 == 0 else 0) ^ jnp.arange(bands, dtype=jnp.int32)
    assert sum(CHUNKS) == pair_count
    plan = [(sum(CHUNKS[:chunk]), pairs) for chunk, pairs in enumerate(CHUNKS)]
    def swap(value, step):
        return lax.ppermute(value, "band", [(band, band ^ step) for band in range(bands)])

    def payloads_of(chunk):
        start, pairs = plan[chunk]
        place, shape = (0, start * fields), (1, rows, pairs * fields)
        return [lax.dynamic_slice(coeffs, (which, *place), shape)[0] for which in (parity, 1 - parity)]

    def redistribute(grid):
        return lax.all_to_all(grid.reshape(sets, fields // sets, -1, lats), "mset", 0, 0)

    def spread(mine, near):
        held = [mine, near]
        for bit in [2**power for power in range(1, bands.bit_length() - 1)]:
            held.append(swap(jnp.concatenate(held), bit))
        return held

    near, far, own_rows = {}, {}, {}

    def send_direct(payload):
        far[0] = [payload[0]] + [swap(payload[step % 2], step) for step in range(1, bands)]
        near[0] = far[0][1]

    def send_near(chunk):
        payload = payloads_of(chunk)
        if chunk >= 2:
            earlier = far[chunk - 3] if chunk >= 3 else near[chunk - 1]
            payload, earlier = lax.optimization_barrier((payload, earlier))
            if chunk >= 3:
                far[chunk - 3] = earlier
            else:
                near[chunk - 1] = earlier
        own_rows[chunk] = payload[0]
        near[chunk] = swap(payload[1], 1)

    def send_far(chunk, after=None):
        parts = [own_rows[chunk], near[chunk]]
        if after is not None:
            parts, after = lax.optimization_barrier((parts, after))
        far[chunk] = spread(*parts)
        return after

    first_rows = payloads_of(0)
    coeffs, first_rows = lax.optimization_barrier((coeffs, first_rows))
    send_direct(first_rows)
    send_near(1)
    send_near(2)
    send_far(1)
    out, written, sums = None, 0, []

    def write():
        nonlocal out, written
        first_slot = 2 * plan[GROUPS[written][0]][0]
        parts = [sums[chunk] for chunk in GROUPS[written]]
        out = finish(parts, parity, band_rows, first_slot, 2 * pair_count, out)
        written += 1

    for chunk, (start, pairs) in enumerate(plan):
        if 3 <= chunk + 3 < len(plan):
            send_near(chunk + 3)
        if chunk < 1:
            far[chunk], near[chunk + 2] = lax.optimization_barrier((far[chunk], near[chunk + 2]))
        if 0 < chunk < len(plan) - 0:
            far[chunk], piece = lax.optimization_barrier((far[chunk], piece))
            sums.append((piece, swap(piece, 1)))
        elif chunk > 0:
            sums.append((piece, swap(piece, 1)))
        if chunk in MIRRORED:
            back = MIRRORED[chunk]
            far[chunk], sums[back] = lax.optimization_barrier((far[chunk], sums[back]))
        if chunk == GROUPS[0][-1] + 3:
            write()
            far[chunk], out = lax.optimization_barrier((far[chunk], out))
        blocks = far[chunk]
        if rows % 16:
            stacked = jnp.concatenate(blocks).reshape(bands, rows, -1)
            blocks = [jnp.take(stacked, me ^ jnp.arange(bands), axis=0).reshape(bands * rows, -1)]
        own = parity_sums(
            blocks, rows if rows % 16 == 0 else depth, order, first, total, legendre, start, pairs, fields
        )
        if chunk + 2 < len(plan):
            own = send_far(chunk + 2, own)
        piece = redistribute(own)
    sums.append((piece, swap(piece, 1)))
    while written < len(GROUPS):
        write()
    return out


def solution(mesh):
    in_specs = (P(None, "band", "mset"), P("mset", None, "band"), P("mset"), P("band"))
    out_specs = P("mset", None, "band")
    return jax.shard_map(shards, mesh=mesh, in_specs=in_specs, out_specs=out_specs, check_vma=False)
```

```python
import functools

import jax
import jax.numpy as jnp
from jax import lax
from jax.experimental import pallas as pl
from jax.experimental.pallas import tpu as pltpu
from jax.sharding import PartitionSpec as P

TRUNC = 1279
VMEM = 24 * 2**20
CHUNKS = (8, 8, 8, 8, 4, 4)
MIRRORED = {3: 0, 4: 1, 5: 2}
GROUPS = ((0, 1), (2, 3), (4, 5))


def owner_limits(wavenumber, parity):
    first = jnp.maximum((TRUNC - wavenumber - parity) // 2 + 1, 0)
    second = jnp.maximum((wavenumber - parity) // 2 + 1, 0)
    return first, first + second


def sums_kernel(rows, fields, start, order, first, total, *refs):
    blocks, (legendre, out, gathered, flipped, sums) = refs[:-5], refs[-5:]
    pairs, depth, lats = legendre.shape
    step = 0
    for part in blocks:
        for row in range(0, part.shape[0], rows):
            place = pl.ds(pl.multiple_of(order[step] * rows, 16), rows)
            gathered[place, :] = part[pl.ds(row, rows), :]
            step += 1
    flipped[...] = gathered[...].T
    row = lax.broadcasted_iota(jnp.int32, (depth, lats), 0)
    for pair in range(pairs):
        here = legendre[pair].astype(jnp.float32)
        in_first = row < first[start + pair]
        in_any = row < total[start + pair]
        part_first = jnp.where(in_first, here, 0.0)
        part_second = jnp.where(in_any, here - part_first, 0.0)
        both = jnp.concatenate([part_first, part_second], axis=1).astype(jnp.bfloat16)
        product = jnp.dot(
            flipped[pair * fields : (pair + 1) * fields, :], both, preferred_element_type=jnp.float32
        )
        sums[:, 2 * pair, :] = product[:, :lats]
        sums[:, 2 * pair + 1, :] = product[:, lats:]
    out[...] = sums[...].astype(out.dtype)


def parity_sums(blocks, rows, order, first, total, legendre, start, pairs, fields):
    columns = blocks[0].shape[1]
    _, depth, lats = legendre.shape
    legendre = legendre[start : start + pairs]
    vmem = pl.BlockSpec(memory_space=pltpu.VMEM)
    scalar = pl.BlockSpec(memory_space=pltpu.SMEM)
    return pl.pallas_call(
        functools.partial(sums_kernel, rows, fields, start),
        in_specs=[scalar] * 3 + [vmem] * (len(blocks) + 1),
        out_specs=vmem,
        scratch_shapes=[
            pltpu.VMEM((depth, columns), jnp.bfloat16),
            pltpu.VMEM((columns, depth), jnp.bfloat16),
            pltpu.VMEM((fields, 2 * pairs, lats), jnp.float32),
        ],
        out_shape=jax.ShapeDtypeStruct((fields, 2 * pairs, lats), jnp.bfloat16),
        compiler_params=pltpu.CompilerParams(vmem_limit_bytes=VMEM),
        cost_estimate=pl.CostEstimate(flops=pairs * 10**11, bytes_accessed=pairs * 100 * 2**20, transcendentals=0),
        name="parity_sums",
    )(order, first, total, *blocks, legendre)


def finish_kernel(first_slot, slots, count, parity, lat_count, *refs):
    owns, partners, (out, result, done) = refs[:count], refs[count : 2 * count], refs[-3:]
    sets, _, width, _ = result.shape
    sign = jnp.where(parity[0] == 0, 1.0, -1.0)
    copies = []
    for group in range(sets):
        slot = 0
        for own, partner in zip(owns, partners):
            grid = partner[group].astype(jnp.float32) + sign * own[group].astype(jnp.float32)
            lat = lax.broadcasted_iota(jnp.int32, grid.shape, 2)
            grid = jnp.where(lat < lat_count[0], grid, 0.0)
            result[group, :, slot : slot + own.shape[2], :] = grid.astype(result.dtype)
            slot += own.shape[2]
        target = out.at[:, pl.ds(group * slots + first_slot, width), :]
        copies.append(pltpu.make_async_copy(result.at[group], target, done.at[group]))
        copies[-1].start()
    for copy in copies:
        copy.wait()


def finish(halves, parity, lat_count, first_slot, slots, out):
    owns, partners = zip(*halves)
    sets, fields, _, lats = owns[0].shape
    width = sum(own.shape[2] for own in owns)
    vmem = pl.BlockSpec(memory_space=pltpu.VMEM)
    hbm = pl.BlockSpec(memory_space=pltpu.HBM)
    scalar = pl.BlockSpec(memory_space=pltpu.SMEM)
    held = [] if out is None else [out]
    return pl.pallas_call(
        functools.partial(finish_kernel, first_slot, slots, len(owns)),
        in_specs=[scalar] * 2 + [vmem] * (2 * len(owns)) + [hbm] * len(held),
        out_specs=hbm,
        scratch_shapes=[
            pltpu.VMEM((sets, fields, width, lats), jnp.bfloat16),
            pltpu.SemaphoreType.DMA((sets,)),
        ],
        out_shape=jax.ShapeDtypeStruct((fields, sets * slots, lats), jnp.bfloat16),
        input_output_aliases={2 + 2 * len(owns): 0} if held else {},
        compiler_params=pltpu.CompilerParams(vmem_limit_bytes=VMEM),
        name="finish",
    )(parity.reshape(1), lat_count, *owns, *partners, *held)


def shards(coeffs, legendre, wavenumber, band_rows):
    bands = lax.axis_size("band")
    sets = lax.axis_size("mset")
    me = lax.axis_index("band")
    parity = me % 2
    pair_count, depth, lats = legendre.shape
    rows = coeffs.shape[1]
    fields = coeffs.shape[2] // pair_count
    first, total = owner_limits(wavenumber, parity)
    order = (me if rows % 16 == 0 else 0) ^ jnp.arange(bands, dtype=jnp.int32)
    assert sum(CHUNKS) == pair_count
    plan = [(sum(CHUNKS[:chunk]), pairs) for chunk, pairs in enumerate(CHUNKS)]
    def swap(value, step):
        return lax.ppermute(value, "band", [(band, band ^ step) for band in range(bands)])

    def payloads_of(chunk):
        start, pairs = plan[chunk]
        place, shape = (0, start * fields), (1, rows, pairs * fields)
        return [lax.dynamic_slice(coeffs, (which, *place), shape)[0] for which in (parity, 1 - parity)]

    def redistribute(grid):
        return lax.all_to_all(grid.reshape(sets, fields // sets, -1, lats), "mset", 0, 0)

    def spread(mine, near):
        held = [mine, near]
        for bit in [2**power for power in range(1, bands.bit_length() - 1)]:
            held.append(swap(jnp.concatenate(held), bit))
        return held

    near, far, own_rows = {}, {}, {}

    def send_direct(payload):
        far[0] = [payload[0]] + [swap(payload[step % 2], step) for step in range(1, bands)]
        near[0] = far[0][1]

    def send_near(chunk):
        payload = payloads_of(chunk)
        if chunk >= 2:
            earlier = far[chunk - 3] if chunk >= 3 else near[chunk - 1]
            payload, earlier = lax.optimization_barrier((payload, earlier))
            if chunk >= 3:
                far[chunk - 3] = earlier
            else:
                near[chunk - 1] = earlier
        own_rows[chunk] = payload[0]
        near[chunk] = swap(payload[1], 1)

    def send_far(chunk, after=None):
        parts = [own_rows[chunk], near[chunk]]
        if after is not None:
            parts, after = lax.optimization_barrier((parts, after))
        far[chunk] = spread(*parts)
        return after

    first_rows = payloads_of(0)
    coeffs, first_rows = lax.optimization_barrier((coeffs, first_rows))
    send_direct(first_rows)
    send_near(1)
    send_near(2)
    send_far(1)
    out, written, sums = None, 0, []

    def write():
        nonlocal out, written
        first_slot = 2 * plan[GROUPS[written][0]][0]
        parts = [sums[chunk] for chunk in GROUPS[written]]
        out = finish(parts, parity, band_rows, first_slot, 2 * pair_count, out)
        written += 1

    for chunk, (start, pairs) in enumerate(plan):
        if 3 <= chunk + 3 < len(plan):
            send_near(chunk + 3)
        if chunk < 1:
            far[chunk], near[chunk + 2] = lax.optimization_barrier((far[chunk], near[chunk + 2]))
        if 0 < chunk < len(plan) - 0:
            far[chunk], piece = lax.optimization_barrier((far[chunk], piece))
            sums.append((piece, swap(piece, 1)))
        elif chunk > 0:
            sums.append((piece, swap(piece, 1)))
        if chunk in MIRRORED:
            back = MIRRORED[chunk]
            far[chunk], sums[back] = lax.optimization_barrier((far[chunk], sums[back]))
        if chunk == GROUPS[0][-1] + 3:
            write()
            far[chunk], out = lax.optimization_barrier((far[chunk], out))
        blocks = far[chunk]
        if rows % 16:
            stacked = jnp.concatenate(blocks).reshape(bands, rows, -1)
            blocks = [jnp.take(stacked, me ^ jnp.arange(bands), axis=0).reshape(bands * rows, -1)]
        own = parity_sums(
            blocks, rows if rows % 16 == 0 else depth, order, first, total, legendre, start, pairs, fields
        )
        if chunk + 2 < len(plan):
            own = send_far(chunk + 2, own)
        piece = redistribute(own)
    sums.append((piece, swap(piece, 1)))
    while written < len(GROUPS):
        write()
    return out


def solution(mesh):
    in_specs = (P(None, "band", "mset"), P("mset", None, "band"), P("mset"), P("band"))
    out_specs = P("mset", None, "band")
    return jax.shard_map(shards, mesh=mesh, in_specs=in_specs, out_specs=out_specs, check_vma=False)
```

```python
import functools

import jax
import jax.numpy as jnp
from jax import lax
from jax.experimental import pallas as pl
from jax.experimental.pallas import tpu as pltpu
from jax.sharding import PartitionSpec as P

TRUNC = 1279
VMEM = 24 * 2**20
CHUNKS = (8, 8, 8, 8, 4, 4)
MIRRORED = {2: 0, 4: 1, 5: 2}
GROUPS = ((0, 1), (2, 3), (4, 5))


def owner_limits(wavenumber, parity):
    first = jnp.maximum((TRUNC - wavenumber - parity) // 2 + 1, 0)
    second = jnp.maximum((wavenumber - parity) // 2 + 1, 0)
    return first, first + second


def sums_kernel(rows, fields, start, order, first, total, *refs):
    blocks, (legendre, out, gathered, flipped, sums) = refs[:-5], refs[-5:]
    pairs, depth, lats = legendre.shape
    step = 0
    for part in blocks:
        for row in range(0, part.shape[0], rows):
            place = pl.ds(pl.multiple_of(order[step] * rows, 16), rows)
            gathered[place, :] = part[pl.ds(row, rows), :]
            step += 1
    flipped[...] = gathered[...].T
    row = lax.broadcasted_iota(jnp.int32, (depth, lats), 0)
    for pair in range(pairs):
        here = legendre[pair].astype(jnp.float32)
        in_first = row < first[start + pair]
        in_any = row < total[start + pair]
        part_first = jnp.where(in_first, here, 0.0)
        part_second = jnp.where(in_any, here - part_first, 0.0)
        both = jnp.concatenate([part_first, part_second], axis=1).astype(jnp.bfloat16)
        product = jnp.dot(
            flipped[pair * fields : (pair + 1) * fields, :], both, preferred_element_type=jnp.float32
        )
        sums[:, 2 * pair, :] = product[:, :lats]
        sums[:, 2 * pair + 1, :] = product[:, lats:]
    out[...] = sums[...].astype(out.dtype)


def parity_sums(blocks, rows, order, first, total, legendre, start, pairs, fields):
    columns = blocks[0].shape[1]
    _, depth, lats = legendre.shape
    legendre = legendre[start : start + pairs]
    vmem = pl.BlockSpec(memory_space=pltpu.VMEM)
    scalar = pl.BlockSpec(memory_space=pltpu.SMEM)
    return pl.pallas_call(
        functools.partial(sums_kernel, rows, fields, start),
        in_specs=[scalar] * 3 + [vmem] * (len(blocks) + 1),
        out_specs=vmem,
        scratch_shapes=[
            pltpu.VMEM((depth, columns), jnp.bfloat16),
            pltpu.VMEM((columns, depth), jnp.bfloat16),
            pltpu.VMEM((fields, 2 * pairs, lats), jnp.float32),
        ],
        out_shape=jax.ShapeDtypeStruct((fields, 2 * pairs, lats), jnp.bfloat16),
        compiler_params=pltpu.CompilerParams(vmem_limit_bytes=VMEM),
        cost_estimate=pl.CostEstimate(flops=pairs * 10**11, bytes_accessed=pairs * 100 * 2**20, transcendentals=0),
        name="parity_sums",
    )(order, first, total, *blocks, legendre)


def finish_kernel(first_slot, slots, count, parity, lat_count, *refs):
    owns, partners, (out, result, done) = refs[:count], refs[count : 2 * count], refs[-3:]
    sets, _, width, _ = result.shape
    sign = jnp.where(parity[0] == 0, 1.0, -1.0)
    copies = []
    for group in range(sets):
        slot = 0
        for own, partner in zip(owns, partners):
            grid = partner[group].astype(jnp.float32) + sign * own[group].astype(jnp.float32)
            lat = lax.broadcasted_iota(jnp.int32, grid.shape, 2)
            grid = jnp.where(lat < lat_count[0], grid, 0.0)
            result[group, :, slot : slot + own.shape[2], :] = grid.astype(result.dtype)
            slot += own.shape[2]
        target = out.at[:, pl.ds(group * slots + first_slot, width), :]
        copies.append(pltpu.make_async_copy(result.at[group], target, done.at[group]))
        copies[-1].start()
    for copy in copies:
        copy.wait()


def finish(halves, parity, lat_count, first_slot, slots, out):
    owns, partners = zip(*halves)
    sets, fields, _, lats = owns[0].shape
    width = sum(own.shape[2] for own in owns)
    vmem = pl.BlockSpec(memory_space=pltpu.VMEM)
    hbm = pl.BlockSpec(memory_space=pltpu.HBM)
    scalar = pl.BlockSpec(memory_space=pltpu.SMEM)
    held = [] if out is None else [out]
    return pl.pallas_call(
        functools.partial(finish_kernel, first_slot, slots, len(owns)),
        in_specs=[scalar] * 2 + [vmem] * (2 * len(owns)) + [hbm] * len(held),
        out_specs=hbm,
        scratch_shapes=[
            pltpu.VMEM((sets, fields, width, lats), jnp.bfloat16),
            pltpu.SemaphoreType.DMA((sets,)),
        ],
        out_shape=jax.ShapeDtypeStruct((fields, sets * slots, lats), jnp.bfloat16),
        input_output_aliases={2 + 2 * len(owns): 0} if held else {},
        compiler_params=pltpu.CompilerParams(vmem_limit_bytes=VMEM),
        name="finish",
    )(parity.reshape(1), lat_count, *owns, *partners, *held)


def shards(coeffs, legendre, wavenumber, band_rows):
    bands = lax.axis_size("band")
    sets = lax.axis_size("mset")
    me = lax.axis_index("band")
    parity = me % 2
    pair_count, depth, lats = legendre.shape
    rows = coeffs.shape[1]
    fields = coeffs.shape[2] // pair_count
    first, total = owner_limits(wavenumber, parity)
    order = (me if rows % 16 == 0 else 0) ^ jnp.arange(bands, dtype=jnp.int32)
    assert sum(CHUNKS) == pair_count
    plan = [(sum(CHUNKS[:chunk]), pairs) for chunk, pairs in enumerate(CHUNKS)]
    def swap(value, step):
        return lax.ppermute(value, "band", [(band, band ^ step) for band in range(bands)])

    def payloads_of(chunk):
        start, pairs = plan[chunk]
        place, shape = (0, start * fields), (1, rows, pairs * fields)
        return [lax.dynamic_slice(coeffs, (which, *place), shape)[0] for which in (parity, 1 - parity)]

    def redistribute(grid):
        return lax.all_to_all(grid.reshape(sets, fields // sets, -1, lats), "mset", 0, 0)

    def spread(mine, near):
        held = [mine, near]
        for bit in [2**power for power in range(1, bands.bit_length() - 1)]:
            held.append(swap(jnp.concatenate(held), bit))
        return held

    near, far, own_rows = {}, {}, {}

    def send_direct(payload):
        far[0] = [payload[0]] + [swap(payload[step % 2], step) for step in range(1, bands)]
        near[0] = far[0][1]

    def send_near(chunk):
        payload = payloads_of(chunk)
        if chunk >= 2:
            earlier = far[chunk - 3] if chunk >= 3 else near[chunk - 1]
            payload, earlier = lax.optimization_barrier((payload, earlier))
            if chunk >= 3:
                far[chunk - 3] = earlier
            else:
                near[chunk - 1] = earlier
        own_rows[chunk] = payload[0]
        near[chunk] = swap(payload[1], 1)

    def send_far(chunk, after=None):
        parts = [own_rows[chunk], near[chunk]]
        if after is not None:
            parts, after = lax.optimization_barrier((parts, after))
        far[chunk] = spread(*parts)
        return after

    first_rows = payloads_of(0)
    coeffs, first_rows = lax.optimization_barrier((coeffs, first_rows))
    send_direct(first_rows)
    send_near(1)
    send_near(2)
    send_far(1)
    out, written, sums = None, 0, []

    def write():
        nonlocal out, written
        first_slot = 2 * plan[GROUPS[written][0]][0]
        parts = [sums[chunk] for chunk in GROUPS[written]]
        out = finish(parts, parity, band_rows, first_slot, 2 * pair_count, out)
        written += 1

    for chunk, (start, pairs) in enumerate(plan):
        if 3 <= chunk + 3 < len(plan):
            send_near(chunk + 3)
        if chunk < 1:
            far[chunk], near[chunk + 2] = lax.optimization_barrier((far[chunk], near[chunk + 2]))
        if 0 < chunk < len(plan) - 0:
            far[chunk], piece = lax.optimization_barrier((far[chunk], piece))
            sums.append((piece, swap(piece, 1)))
        elif chunk > 0:
            sums.append((piece, swap(piece, 1)))
        if chunk in MIRRORED:
            back = MIRRORED[chunk]
            far[chunk], sums[back] = lax.optimization_barrier((far[chunk], sums[back]))
        if chunk == GROUPS[0][-1] + 3:
            write()
            far[chunk], out = lax.optimization_barrier((far[chunk], out))
        blocks = far[chunk]
        if rows % 16:
            stacked = jnp.concatenate(blocks).reshape(bands, rows, -1)
            blocks = [jnp.take(stacked, me ^ jnp.arange(bands), axis=0).reshape(bands * rows, -1)]
        own = parity_sums(
            blocks, rows if rows % 16 == 0 else depth, order, first, total, legendre, start, pairs, fields
        )
        if chunk + 2 < len(plan):
            own = send_far(chunk + 2, own)
        piece = redistribute(own)
    sums.append((piece, swap(piece, 1)))
    while written < len(GROUPS):
        write()
    return out


def solution(mesh):
    in_specs = (P(None, "band", "mset"), P("mset", None, "band"), P("mset"), P("band"))
    out_specs = P("mset", None, "band")
    return jax.shard_map(shards, mesh=mesh, in_specs=in_specs, out_specs=out_specs, check_vma=False)
```

```python
import functools

import jax
import jax.numpy as jnp
from jax import lax
from jax.experimental import pallas as pl
from jax.experimental.pallas import tpu as pltpu
from jax.sharding import PartitionSpec as P

TRUNC = 1279
VMEM = 24 * 2**20
CHUNKS = (8, 8, 8, 8, 4, 4)
MIRRORED = {3: 0, 4: 1, 5: 2}
GROUPS = ((0, 1), (2, 3), (4, 5))


def owner_limits(wavenumber, parity):
    first = jnp.maximum((TRUNC - wavenumber - parity) // 2 + 1, 0)
    second = jnp.maximum((wavenumber - parity) // 2 + 1, 0)
    return first, first + second


def sums_kernel(rows, fields, start, order, first, total, *refs):
    blocks, (legendre, out, gathered, flipped, sums) = refs[:-5], refs[-5:]
    pairs, depth, lats = legendre.shape
    step = 0
    for part in blocks:
        for row in range(0, part.shape[0], rows):
            place = pl.ds(pl.multiple_of(order[step] * rows, 16), rows)
            gathered[place, :] = part[pl.ds(row, rows), :]
            step += 1
    flipped[...] = gathered[...].T
    row = lax.broadcasted_iota(jnp.int32, (depth, lats), 0)
    for pair in range(pairs):
        here = legendre[pair].astype(jnp.float32)
        in_first = row < first[start + pair]
        in_any = row < total[start + pair]
        part_first = jnp.where(in_first, here, 0.0)
        part_second = jnp.where(in_any, here - part_first, 0.0)
        both = jnp.concatenate([part_first, part_second], axis=1).astype(jnp.bfloat16)
        product = jnp.dot(
            flipped[pair * fields : (pair + 1) * fields, :], both, preferred_element_type=jnp.float32
        )
        sums[:, 2 * pair, :] = product[:, :lats]
        sums[:, 2 * pair + 1, :] = product[:, lats:]
    out[...] = sums[...].astype(out.dtype)


def parity_sums(blocks, rows, order, first, total, legendre, start, pairs, fields):
    columns = blocks[0].shape[1]
    _, depth, lats = legendre.shape
    legendre = legendre[start : start + pairs]
    vmem = pl.BlockSpec(memory_space=pltpu.VMEM)
    scalar = pl.BlockSpec(memory_space=pltpu.SMEM)
    return pl.pallas_call(
        functools.partial(sums_kernel, rows, fields, start),
        in_specs=[scalar] * 3 + [vmem] * (len(blocks) + 1),
        out_specs=vmem,
        scratch_shapes=[
            pltpu.VMEM((depth, columns), jnp.bfloat16),
            pltpu.VMEM((columns, depth), jnp.bfloat16),
            pltpu.VMEM((fields, 2 * pairs, lats), jnp.float32),
        ],
        out_shape=jax.ShapeDtypeStruct((fields, 2 * pairs, lats), jnp.bfloat16),
        compiler_params=pltpu.CompilerParams(vmem_limit_bytes=VMEM),
        cost_estimate=pl.CostEstimate(flops=pairs * 10**11, bytes_accessed=pairs * 100 * 2**20, transcendentals=0),
        name="parity_sums",
    )(order, first, total, *blocks, legendre)


def finish_kernel(first_slot, slots, count, parity, lat_count, *refs):
    owns, partners, (out, result, done) = refs[:count], refs[count : 2 * count], refs[-3:]
    sets, _, width, _ = result.shape
    sign = jnp.where(parity[0] == 0, 1.0, -1.0)
    copies = []
    for group in range(sets):
        slot = 0
        for own, partner in zip(owns, partners):
            grid = partner[group].astype(jnp.float32) + sign * own[group].astype(jnp.float32)
            lat = lax.broadcasted_iota(jnp.int32, grid.shape, 2)
            grid = jnp.where(lat < lat_count[0], grid, 0.0)
            result[group, :, slot : slot + own.shape[2], :] = grid.astype(result.dtype)
            slot += own.shape[2]
        target = out.at[:, pl.ds(group * slots + first_slot, width), :]
        copies.append(pltpu.make_async_copy(result.at[group], target, done.at[group]))
        copies[-1].start()
    for copy in copies:
        copy.wait()


def finish(halves, parity, lat_count, first_slot, slots, out):
    owns, partners = zip(*halves)
    sets, fields, _, lats = owns[0].shape
    width = sum(own.shape[2] for own in owns)
    vmem = pl.BlockSpec(memory_space=pltpu.VMEM)
    hbm = pl.BlockSpec(memory_space=pltpu.HBM)
    scalar = pl.BlockSpec(memory_space=pltpu.SMEM)
    held = [] if out is None else [out]
    return pl.pallas_call(
        functools.partial(finish_kernel, first_slot, slots, len(owns)),
        in_specs=[scalar] * 2 + [vmem] * (2 * len(owns)) + [hbm] * len(held),
        out_specs=hbm,
        scratch_shapes=[
            pltpu.VMEM((sets, fields, width, lats), jnp.bfloat16),
            pltpu.SemaphoreType.DMA((sets,)),
        ],
        out_shape=jax.ShapeDtypeStruct((fields, sets * slots, lats), jnp.bfloat16),
        input_output_aliases={2 + 2 * len(owns): 0} if held else {},
        compiler_params=pltpu.CompilerParams(vmem_limit_bytes=VMEM),
        name="finish",
    )(parity.reshape(1), lat_count, *owns, *partners, *held)


def shards(coeffs, legendre, wavenumber, band_rows):
    bands = lax.axis_size("band")
    sets = lax.axis_size("mset")
    me = lax.axis_index("band")
    parity = me % 2
    pair_count, depth, lats = legendre.shape
    rows = coeffs.shape[1]
    fields = coeffs.shape[2] // pair_count
    first, total = owner_limits(wavenumber, parity)
    order = (me if rows % 16 == 0 else 0) ^ jnp.arange(bands, dtype=jnp.int32)
    assert sum(CHUNKS) == pair_count
    plan = [(sum(CHUNKS[:chunk]), pairs) for chunk, pairs in enumerate(CHUNKS)]
    def swap(value, step):
        return lax.ppermute(value, "band", [(band, band ^ step) for band in range(bands)])

    def payloads_of(chunk, pairs):
        start = plan[chunk][0]
        place, shape = (0, start * fields), (1, rows, pairs * fields)
        return [lax.dynamic_slice(coeffs, (which, *place), shape)[0] for which in (parity, 1 - parity)]

    def redistribute(grid):
        return lax.all_to_all(grid.reshape(sets, fields // sets, -1, lats), "mset", 0, 0)

    def spread(mine, near):
        held = [mine, near]
        for bit in [2**power for power in range(1, bands.bit_length() - 1)]:
            held.append(swap(jnp.concatenate(held), bit))
        return held

    near, far, own_rows = {}, {}, {}

    def send_direct(payload):
        far[0] = [payload[0]] + [swap(payload[step % 2], step) for step in range(1, bands)]
        near[0] = far[0][1]

    def send_near(chunk, after=None):
        both = range(chunk, min(chunk + 2, len(plan)) if chunk == len(plan) - 2 else chunk + 1)
        if chunk in near:
            return after
        payload = payloads_of(chunk, sum(plan[part][1] for part in both))
        if chunk == 2:
            payload, near[1] = lax.optimization_barrier((payload, near[1]))
        elif chunk > 2:
            payload, after = lax.optimization_barrier((payload, after))
        arrived = swap(payload[1], 1)
        for part in both:
            offset, pairs = plan[part][0] - plan[chunk][0], plan[part][1]
            columns = slice(offset * fields, (offset + pairs) * fields)
            own_rows[part], near[part] = payload[0][:, columns], arrived[:, columns]
        return after

    def send_far(chunk, after=None):
        parts = [own_rows[chunk], near[chunk]]
        if after is not None:
            parts, after = lax.optimization_barrier((parts, after))
        far[chunk] = spread(*parts)
        return after

    first_rows = payloads_of(0, plan[0][1])
    coeffs, first_rows = lax.optimization_barrier((coeffs, first_rows))
    send_direct(first_rows)
    send_near(1)
    send_near(2)
    send_far(1)
    out, written, sums = None, 0, []

    def write():
        nonlocal out, written
        first_slot = 2 * plan[GROUPS[written][0]][0]
        parts = [sums[chunk] for chunk in GROUPS[written]]
        out = finish(parts, parity, band_rows, first_slot, 2 * pair_count, out)
        written += 1

    for chunk, (start, pairs) in enumerate(plan):
        if chunk < 1:
            far[chunk], near[chunk + 2] = lax.optimization_barrier((far[chunk], near[chunk + 2]))
        if 0 < chunk < len(plan) - 0:
            far[chunk], piece = lax.optimization_barrier((far[chunk], piece))
            sums.append((piece, swap(piece, 1)))
        elif chunk > 0:
            sums.append((piece, swap(piece, 1)))
        if chunk in MIRRORED:
            back = MIRRORED[chunk]
            far[chunk], sums[back] = lax.optimization_barrier((far[chunk], sums[back]))
        if chunk == GROUPS[0][-1] + 4:
            write()
            far[chunk], out = lax.optimization_barrier((far[chunk], out))
        blocks = far[chunk]
        if rows % 16:
            stacked = jnp.concatenate(blocks).reshape(bands, rows, -1)
            blocks = [jnp.take(stacked, me ^ jnp.arange(bands), axis=0).reshape(bands * rows, -1)]
        own = parity_sums(
            blocks, rows if rows % 16 == 0 else depth, order, first, total, legendre, start, pairs, fields
        )
        if chunk + 3 < len(plan):
            own = send_near(chunk + 3, own)
        if chunk + 2 < len(plan):
            own = send_far(chunk + 2, own)
        piece = redistribute(own)
    sums.append((piece, swap(piece, 1)))
    while written < len(GROUPS):
        write()
    return out


def solution(mesh):
    in_specs = (P(None, "band", "mset"), P("mset", None, "band"), P("mset"), P("band"))
    out_specs = P("mset", None, "band")
    return jax.shard_map(shards, mesh=mesh, in_specs=in_specs, out_specs=out_specs, check_vma=False)
```

```python
import functools

import jax
import jax.numpy as jnp
from jax import lax
from jax.experimental import pallas as pl
from jax.experimental.pallas import tpu as pltpu
from jax.sharding import PartitionSpec as P

TRUNC = 1279
VMEM = 24 * 2**20
CHUNKS = (8, 8, 8, 8, 4, 4)
MIRRORED = {2: 0, 3: 1}
GROUPS = ((0, 1), (2, 3), (4, 5))


def owner_limits(wavenumber, parity):
    first = jnp.maximum((TRUNC - wavenumber - parity) // 2 + 1, 0)
    second = jnp.maximum((wavenumber - parity) // 2 + 1, 0)
    return first, first + second


def sums_kernel(rows, fields, start, order, first, total, *refs):
    blocks, (legendre, out, gathered, flipped, sums) = refs[:-5], refs[-5:]
    pairs, depth, lats = legendre.shape
    step = 0
    for part in blocks:
        for row in range(0, part.shape[0], rows):
            place = pl.ds(pl.multiple_of(order[step] * rows, 16), rows)
            gathered[place, :] = part[pl.ds(row, rows), :]
            step += 1
    flipped[...] = gathered[...].T
    row = lax.broadcasted_iota(jnp.int32, (depth, lats), 0)
    for pair in range(pairs):
        here = legendre[pair].astype(jnp.float32)
        in_first = row < first[start + pair]
        in_any = row < total[start + pair]
        part_first = jnp.where(in_first, here, 0.0)
        part_second = jnp.where(in_any, here - part_first, 0.0)
        both = jnp.concatenate([part_first, part_second], axis=1).astype(jnp.bfloat16)
        product = jnp.dot(
            flipped[pair * fields : (pair + 1) * fields, :], both, preferred_element_type=jnp.float32
        )
        sums[:, 2 * pair, :] = product[:, :lats]
        sums[:, 2 * pair + 1, :] = product[:, lats:]
    out[...] = sums[...].astype(out.dtype)


def parity_sums(blocks, rows, order, first, total, legendre, start, pairs, fields):
    columns = blocks[0].shape[1]
    _, depth, lats = legendre.shape
    legendre = legendre[start : start + pairs]
    vmem = pl.BlockSpec(memory_space=pltpu.VMEM)
    scalar = pl.BlockSpec(memory_space=pltpu.SMEM)
    return pl.pallas_call(
        functools.partial(sums_kernel, rows, fields, start),
        in_specs=[scalar] * 3 + [vmem] * (len(blocks) + 1),
        out_specs=vmem,
        scratch_shapes=[
            pltpu.VMEM((depth, columns), jnp.bfloat16),
            pltpu.VMEM((columns, depth), jnp.bfloat16),
            pltpu.VMEM((fields, 2 * pairs, lats), jnp.float32),
        ],
        out_shape=jax.ShapeDtypeStruct((fields, 2 * pairs, lats), jnp.bfloat16),
        compiler_params=pltpu.CompilerParams(vmem_limit_bytes=VMEM),
        cost_estimate=pl.CostEstimate(flops=pairs * 10**11, bytes_accessed=pairs * 100 * 2**20, transcendentals=0),
        name="parity_sums",
    )(order, first, total, *blocks, legendre)


def finish_kernel(first_slot, slots, count, parity, lat_count, *refs):
    owns, partners, (out, result, done) = refs[:count], refs[count : 2 * count], refs[-3:]
    sets, _, width, _ = result.shape
    sign = jnp.where(parity[0] == 0, 1.0, -1.0)
    copies = []
    for group in range(sets):
        slot = 0
        for own, partner in zip(owns, partners):
            grid = partner[group].astype(jnp.float32) + sign * own[group].astype(jnp.float32)
            lat = lax.broadcasted_iota(jnp.int32, grid.shape, 2)
            grid = jnp.where(lat < lat_count[0], grid, 0.0)
            result[group, :, slot : slot + own.shape[2], :] = grid.astype(result.dtype)
            slot += own.shape[2]
        target = out.at[:, pl.ds(group * slots + first_slot, width), :]
        copies.append(pltpu.make_async_copy(result.at[group], target, done.at[group]))
        copies[-1].start()
    for copy in copies:
        copy.wait()


def finish(halves, parity, lat_count, first_slot, slots, out):
    owns, partners = zip(*halves)
    sets, fields, _, lats = owns[0].shape
    width = sum(own.shape[2] for own in owns)
    vmem = pl.BlockSpec(memory_space=pltpu.VMEM)
    hbm = pl.BlockSpec(memory_space=pltpu.HBM)
    scalar = pl.BlockSpec(memory_space=pltpu.SMEM)
    held = [] if out is None else [out]
    return pl.pallas_call(
        functools.partial(finish_kernel, first_slot, slots, len(owns)),
        in_specs=[scalar] * 2 + [vmem] * (2 * len(owns)) + [hbm] * len(held),
        out_specs=hbm,
        scratch_shapes=[
            pltpu.VMEM((sets, fields, width, lats), jnp.bfloat16),
            pltpu.SemaphoreType.DMA((sets,)),
        ],
        out_shape=jax.ShapeDtypeStruct((fields, sets * slots, lats), jnp.bfloat16),
        input_output_aliases={2 + 2 * len(owns): 0} if held else {},
        compiler_params=pltpu.CompilerParams(vmem_limit_bytes=VMEM),
        name="finish",
    )(parity.reshape(1), lat_count, *owns, *partners, *held)


def shards(coeffs, legendre, wavenumber, band_rows):
    bands = lax.axis_size("band")
    sets = lax.axis_size("mset")
    me = lax.axis_index("band")
    parity = me % 2
    pair_count, depth, lats = legendre.shape
    rows = coeffs.shape[1]
    fields = coeffs.shape[2] // pair_count
    first, total = owner_limits(wavenumber, parity)
    order = (me if rows % 16 == 0 else 0) ^ jnp.arange(bands, dtype=jnp.int32)
    assert sum(CHUNKS) == pair_count
    plan = [(sum(CHUNKS[:chunk]), pairs) for chunk, pairs in enumerate(CHUNKS)]
    def swap(value, step):
        return lax.ppermute(value, "band", [(band, band ^ step) for band in range(bands)])

    def payloads_of(chunk):
        start, pairs = plan[chunk]
        place, shape = (0, start * fields), (1, rows, pairs * fields)
        return [lax.dynamic_slice(coeffs, (which, *place), shape)[0] for which in (parity, 1 - parity)]

    def redistribute(grid):
        return lax.all_to_all(grid.reshape(sets, fields // sets, -1, lats), "mset", 0, 0)

    def spread(mine, near):
        held = [mine, near]
        for bit in [2**power for power in range(1, bands.bit_length() - 1)]:
            held.append(swap(jnp.concatenate(held), bit))
        return held

    near, far, own_rows = {}, {}, {}

    def send_direct(payload):
        far[0] = [payload[0]] + [swap(payload[step % 2], step) for step in range(1, bands)]
        near[0] = far[0][1]

    def send_near(chunk):
        payload = payloads_of(chunk)
        if chunk >= 2:
            earlier = far[chunk - 3] if chunk >= 3 else near[chunk - 1]
            payload, earlier = lax.optimization_barrier((payload, earlier))
            if chunk >= 3:
                far[chunk - 3] = earlier
            else:
                near[chunk - 1] = earlier
        own_rows[chunk] = payload[0]
        near[chunk] = swap(payload[1], 1)

    def send_far(chunk, after=None):
        parts = [own_rows[chunk], near[chunk]]
        if after is not None:
            parts, after = lax.optimization_barrier((parts, after))
        far[chunk] = spread(*parts)
        return after

    first_rows = payloads_of(0)
    coeffs, first_rows = lax.optimization_barrier((coeffs, first_rows))
    send_direct(first_rows)
    send_near(1)
    send_near(2)
    send_far(1)
    out, written, sums = None, 0, []

    def write():
        nonlocal out, written
        first_slot = 2 * plan[GROUPS[written][0]][0]
        parts = [sums[chunk] for chunk in GROUPS[written]]
        out = finish(parts, parity, band_rows, first_slot, 2 * pair_count, out)
        written += 1

    for chunk, (start, pairs) in enumerate(plan):
        if 3 <= chunk + 3 < len(plan):
            send_near(chunk + 3)
        if chunk < 1:
            far[chunk], near[chunk + 2] = lax.optimization_barrier((far[chunk], near[chunk + 2]))
        if 0 < chunk < len(plan) - 0:
            far[chunk], piece = lax.optimization_barrier((far[chunk], piece))
            sums.append((piece, swap(piece, 1)))
        elif chunk > 0:
            sums.append((piece, swap(piece, 1)))
        if chunk in MIRRORED:
            back = MIRRORED[chunk]
            far[chunk], sums[back] = lax.optimization_barrier((far[chunk], sums[back]))
        if chunk == GROUPS[0][-1] + 3:
            write()
            far[chunk], out = lax.optimization_barrier((far[chunk], out))
        blocks = far[chunk]
        if rows % 16:
            stacked = jnp.concatenate(blocks).reshape(bands, rows, -1)
            blocks = [jnp.take(stacked, me ^ jnp.arange(bands), axis=0).reshape(bands * rows, -1)]
        own = parity_sums(
            blocks, rows if rows % 16 == 0 else depth, order, first, total, legendre, start, pairs, fields
        )
        if chunk + 2 < len(plan):
            own = send_far(chunk + 2, own)
        piece = redistribute(own)
    sums.append((piece, swap(piece, 1)))
    while written < len(GROUPS):
        write()
    return out


def solution(mesh):
    in_specs = (P(None, "band", "mset"), P("mset", None, "band"), P("mset"), P("band"))
    out_specs = P("mset", None, "band")
    return jax.shard_map(shards, mesh=mesh, in_specs=in_specs, out_specs=out_specs, check_vma=False)
```

```python
import functools

import jax
import jax.numpy as jnp
from jax import lax
from jax.experimental import pallas as pl
from jax.experimental.pallas import tpu as pltpu
from jax.sharding import PartitionSpec as P

TRUNC = 1279
VMEM = 24 * 2**20
CHUNKS = (8, 8, 8, 8, 4, 4)
MIRRORED = {2: 0, 3: 1, 5: 2}
GROUPS = ((0, 1), (2, 3), (4, 5))


def owner_limits(wavenumber, parity):
    first = jnp.maximum((TRUNC - wavenumber - parity) // 2 + 1, 0)
    second = jnp.maximum((wavenumber - parity) // 2 + 1, 0)
    return first, first + second


def sums_kernel(rows, fields, start, order, first, total, *refs):
    blocks, (legendre, out, gathered, flipped, sums) = refs[:-5], refs[-5:]
    pairs, depth, lats = legendre.shape
    step = 0
    for part in blocks:
        for row in range(0, part.shape[0], rows):
            place = pl.ds(pl.multiple_of(order[step] * rows, 16), rows)
            gathered[place, :] = part[pl.ds(row, rows), :]
            step += 1
    flipped[...] = gathered[...].T
    row = lax.broadcasted_iota(jnp.int32, (depth, lats), 0)
    for pair in range(pairs):
        here = legendre[pair].astype(jnp.float32)
        in_first = row < first[start + pair]
        in_any = row < total[start + pair]
        part_first = jnp.where(in_first, here, 0.0)
        part_second = jnp.where(in_any, here - part_first, 0.0)
        both = jnp.concatenate([part_first, part_second], axis=1).astype(jnp.bfloat16)
        product = jnp.dot(
            flipped[pair * fields : (pair + 1) * fields, :], both, preferred_element_type=jnp.float32
        )
        sums[:, 2 * pair, :] = product[:, :lats]
        sums[:, 2 * pair + 1, :] = product[:, lats:]
    out[...] = sums[...].astype(out.dtype)


def parity_sums(blocks, rows, order, first, total, legendre, start, pairs, fields):
    columns = blocks[0].shape[1]
    _, depth, lats = legendre.shape
    legendre = legendre[start : start + pairs]
    vmem = pl.BlockSpec(memory_space=pltpu.VMEM)
    scalar = pl.BlockSpec(memory_space=pltpu.SMEM)
    return pl.pallas_call(
        functools.partial(sums_kernel, rows, fields, start),
        in_specs=[scalar] * 3 + [vmem] * (len(blocks) + 1),
        out_specs=vmem,
        scratch_shapes=[
            pltpu.VMEM((depth, columns), jnp.bfloat16),
            pltpu.VMEM((columns, depth), jnp.bfloat16),
            pltpu.VMEM((fields, 2 * pairs, lats), jnp.float32),
        ],
        out_shape=jax.ShapeDtypeStruct((fields, 2 * pairs, lats), jnp.bfloat16),
        compiler_params=pltpu.CompilerParams(vmem_limit_bytes=VMEM),
        cost_estimate=pl.CostEstimate(flops=pairs * 10**11, bytes_accessed=pairs * 100 * 2**20, transcendentals=0),
        name="parity_sums",
    )(order, first, total, *blocks, legendre)


def finish_kernel(first_slot, slots, count, parity, lat_count, *refs):
    owns, partners, (out, result, done) = refs[:count], refs[count : 2 * count], refs[-3:]
    sets, _, width, _ = result.shape
    sign = jnp.where(parity[0] == 0, 1.0, -1.0)
    copies = []
    for group in range(sets):
        slot = 0
        for own, partner in zip(owns, partners):
            grid = partner[group].astype(jnp.float32) + sign * own[group].astype(jnp.float32)
            lat = lax.broadcasted_iota(jnp.int32, grid.shape, 2)
            grid = jnp.where(lat < lat_count[0], grid, 0.0)
            result[group, :, slot : slot + own.shape[2], :] = grid.astype(result.dtype)
            slot += own.shape[2]
        target = out.at[:, pl.ds(group * slots + first_slot, width), :]
        copies.append(pltpu.make_async_copy(result.at[group], target, done.at[group]))
        copies[-1].start()
    for copy in copies:
        copy.wait()


def finish(halves, parity, lat_count, first_slot, slots, out):
    owns, partners = zip(*halves)
    sets, fields, _, lats = owns[0].shape
    width = sum(own.shape[2] for own in owns)
    vmem = pl.BlockSpec(memory_space=pltpu.VMEM)
    hbm = pl.BlockSpec(memory_space=pltpu.HBM)
    scalar = pl.BlockSpec(memory_space=pltpu.SMEM)
    held = [] if out is None else [out]
    return pl.pallas_call(
        functools.partial(finish_kernel, first_slot, slots, len(owns)),
        in_specs=[scalar] * 2 + [vmem] * (2 * len(owns)) + [hbm] * len(held),
        out_specs=hbm,
        scratch_shapes=[
            pltpu.VMEM((sets, fields, width, lats), jnp.bfloat16),
            pltpu.SemaphoreType.DMA((sets,)),
        ],
        out_shape=jax.ShapeDtypeStruct((fields, sets * slots, lats), jnp.bfloat16),
        input_output_aliases={2 + 2 * len(owns): 0} if held else {},
        compiler_params=pltpu.CompilerParams(vmem_limit_bytes=VMEM),
        name="finish",
    )(parity.reshape(1), lat_count, *owns, *partners, *held)


def shards(coeffs, legendre, wavenumber, band_rows):
    bands = lax.axis_size("band")
    sets = lax.axis_size("mset")
    me = lax.axis_index("band")
    parity = me % 2
    pair_count, depth, lats = legendre.shape
    rows = coeffs.shape[1]
    fields = coeffs.shape[2] // pair_count
    first, total = owner_limits(wavenumber, parity)
    order = (me if rows % 16 == 0 else 0) ^ jnp.arange(bands, dtype=jnp.int32)
    assert sum(CHUNKS) == pair_count
    plan = [(sum(CHUNKS[:chunk]), pairs) for chunk, pairs in enumerate(CHUNKS)]
    def swap(value, step):
        return lax.ppermute(value, "band", [(band, band ^ step) for band in range(bands)])

    def payloads_of(chunk):
        start, pairs = plan[chunk]
        place, shape = (0, start * fields), (1, rows, pairs * fields)
        return [lax.dynamic_slice(coeffs, (which, *place), shape)[0] for which in (parity, 1 - parity)]

    def redistribute(grid):
        return lax.all_to_all(grid.reshape(sets, fields // sets, -1, lats), "mset", 0, 0)

    def spread(mine, near):
        held = [mine, near]
        for bit in [2**power for power in range(1, bands.bit_length() - 1)]:
            held.append(swap(jnp.concatenate(held), bit))
        return held

    near, far, own_rows = {}, {}, {}

    def send_direct(payload):
        far[0] = [payload[0]] + [swap(payload[step % 2], step) for step in range(1, bands)]
        near[0] = far[0][1]

    def send_near(chunk):
        payload = payloads_of(chunk)
        if chunk >= 2:
            earlier = far[chunk - 3] if chunk >= 3 else near[chunk - 1]
            payload, earlier = lax.optimization_barrier((payload, earlier))
            if chunk >= 3:
                far[chunk - 3] = earlier
            else:
                near[chunk - 1] = earlier
        own_rows[chunk] = payload[0]
        near[chunk] = swap(payload[1], 1)

    def send_far(chunk, after=None):
        parts = [own_rows[chunk], near[chunk]]
        if after is not None:
            parts, after = lax.optimization_barrier((parts, after))
        far[chunk] = spread(*parts)
        return after

    first_rows = payloads_of(0)
    coeffs, first_rows = lax.optimization_barrier((coeffs, first_rows))
    send_direct(first_rows)
    send_near(1)
    send_near(2)
    send_far(1)
    out, written, sums = None, 0, []

    def write():
        nonlocal out, written
        first_slot = 2 * plan[GROUPS[written][0]][0]
        parts = [sums[chunk] for chunk in GROUPS[written]]
        out = finish(parts, parity, band_rows, first_slot, 2 * pair_count, out)
        written += 1

    for chunk, (start, pairs) in enumerate(plan):
        if 3 <= chunk + 3 < len(plan):
            send_near(chunk + 3)
        if chunk < 1:
            far[chunk], near[chunk + 2] = lax.optimization_barrier((far[chunk], near[chunk + 2]))
        if 0 < chunk < len(plan) - 0:
            far[chunk], piece = lax.optimization_barrier((far[chunk], piece))
            sums.append((piece, swap(piece, 1)))
        elif chunk > 0:
            sums.append((piece, swap(piece, 1)))
        if chunk in MIRRORED:
            back = MIRRORED[chunk]
            far[chunk], sums[back] = lax.optimization_barrier((far[chunk], sums[back]))
        if chunk == GROUPS[0][-1] + 4:
            write()
            far[chunk], out = lax.optimization_barrier((far[chunk], out))
        blocks = far[chunk]
        if rows % 16:
            stacked = jnp.concatenate(blocks).reshape(bands, rows, -1)
            blocks = [jnp.take(stacked, me ^ jnp.arange(bands), axis=0).reshape(bands * rows, -1)]
        own = parity_sums(
            blocks, rows if rows % 16 == 0 else depth, order, first, total, legendre, start, pairs, fields
        )
        if chunk + 2 < len(plan):
            own = send_far(chunk + 2, own)
        piece = redistribute(own)
    sums.append((piece, swap(piece, 1)))
    while written < len(GROUPS):
        write()
    return out


def solution(mesh):
    in_specs = (P(None, "band", "mset"), P("mset", None, "band"), P("mset"), P("band"))
    out_specs = P("mset", None, "band")
    return jax.shard_map(shards, mesh=mesh, in_specs=in_specs, out_specs=out_specs, check_vma=False)
```
